32 devices in a mesh: ctx: 16 (over z, y, core), head: 2 (over x).
Axes of the slice: x: 2, y: 2, z: 4, core: 2. Of those that a mesh axis runs over, the one named last changes fastest.
Arguments:
- queries: bfloat16 [8192, 512], P('ctx', 'head'), may hold values from -256 to 256
- rotated_key_rows: bfloat16 [8192, 256], P('ctx', 'head'), may hold values from -8 to 8
- value_head_rows: bfloat16 [8192, 256], P('ctx', 'head'), may hold values from -24 to 24
- stride_offset: int32 [4], P('head'), may hold values from 0 to 7
- w_out: bfloat16 [512, 4096], P('head'), may hold values from -0.25 to 0.25
- grad_out: bfloat16 [8192, 4096], P('ctx', 'head'), may hold values from -6 to 6
Outputs:
- layer_out: bfloat16 [8192, 4096], P('ctx', 'head')
- grad_queries: bfloat16 [8192, 512], P('ctx', 'head')
- key_gradient: bfloat16 [8192, 256], P('ctx', 'head')
- value_gradient: bfloat16 [8192, 256], P('ctx', 'head')
- grad_w_out: bfloat16 [512, 4096], P('head', 'ctx')
The draws below stay inside these ranges and needn't reach their ends.
All inputs are finite; a program needn't handle non-finite values.
Results may differ from the reference program's by a relative error of at most 0.033.
Values may be sent and summed in bfloat16 or wider, within the bound.
No kernel may reach another device: no remote copies, remote signals or barrier semaphores. Data moves between devices by JAX's collectives and lax.ppermute only.
A program may use at most 128 MiB of HBM per device.

```python
import math
import jax
import jax.numpy as jnp
from jax import lax

D = 4096
HEAD_SIZE = 128
QUERY_PER_KEY = 2
BLOCK_TOKENS = 64
LOCAL = 16
STRIDE = 8
TOKENS_PER_INDEX = 512
SEQUENCE_TOKENS = 8192
KEY_VALUE_HEADS = 2
HQ = 4
N_CTX = 16
N_HEAD = 2


def joint_draw(key):
    key_random_seed = jax.random.fold_in(key, 7)
    query_random_seed = jax.random.fold_in(key, 9)
    key_head_rows = jnp.clip(jax.random.normal(key_random_seed, (SEQUENCE_TOKENS, KEY_VALUE_HEADS, HEAD_SIZE), jnp.float32), -4.0, 4.0)
    query_head_rows = jnp.clip(1.5 * jax.random.normal(query_random_seed, (SEQUENCE_TOKENS, KEY_VALUE_HEADS, QUERY_PER_KEY, HEAD_SIZE), jnp.float32), -9.0, 9.0)
    return (query_head_rows.reshape(SEQUENCE_TOKENS, KEY_VALUE_HEADS * QUERY_PER_KEY * HEAD_SIZE), key_head_rows.reshape(SEQUENCE_TOKENS, KEY_VALUE_HEADS * HEAD_SIZE))


def draw_queries(key, part):
    return joint_draw(key)[0].astype(jnp.bfloat16)


def draw_rotated_key_rows(key, part):
    return joint_draw(key)[1].astype(jnp.bfloat16)


def with_ends(drawn, own_key, smallest, top_value):
    shape = drawn.shape
    spot = [jax.random.randint(jax.random.fold_in(own_key, axis), (), 0, shape[axis]) for axis in range(len(shape))]
    drawn = drawn.at[tuple(spot)].set(smallest)
    longest = shape.index(max(shape))
    spot[longest] = (spot[longest] + 1) % shape[longest]
    return drawn.at[tuple(spot)].set(top_value)


def with_spikes(drawn, rng, source, target, shards_of, factor):
    def block_of(dim):
        return (jnp.arange(drawn.shape[dim]) // (drawn.shape[dim] // shards_of)).reshape((-1,) + (1,) * (drawn.ndim - 1 - dim))

    one_side = jax.random.permutation(rng, shards_of)[block_of(target)]
    other_side = (block_of(target) + shards_of // 2) % shards_of
    return jnp.where((block_of(source) == one_side) | (block_of(source) == other_side), factor * drawn, drawn)


def block_scale(own_key, dims, cuts, least, high):
    level, own = 1.0, jax.random.fold_in(own_key, 6)
    for axis_at, blocks in cuts:
        draws = jnp.exp(jax.random.uniform(jax.random.fold_in(own, axis_at), (blocks,), jnp.float32, least / len(cuts), high / len(cuts)))
        level = level * jnp.repeat(draws, dims[axis_at] // blocks).reshape([-1 if axis == axis_at else 1 for axis in range(len(dims))])
    return level


def noise(own_key, shape, width, limit, cuts=(), held_as=jnp.bfloat16):
    entries = width * jax.random.normal(own_key, shape, jnp.float32)
    if cuts:
        entries = entries * block_scale(own_key, shape, cuts, -0.22, 0.18)
    return jnp.clip(entries, -limit, limit).astype(held_as)


def noise_with(key, dims, width, most, pieces, heavy, held_as=jnp.bfloat16):
    values = width * jax.random.normal(key, dims, jnp.float32)
    if pieces:
        values = values * block_scale(key, dims, pieces, -0.22, 0.18)
    return jnp.clip(with_spikes(values, jax.random.fold_in(key, 3), *heavy), -most, most).astype(held_as)


def setup_inputs(seed: int = 0) -> dict:
    key_list = jax.random.split(jax.random.key(seed), 7)
    queries = draw_queries(jax.random.fold_in(key_list[6], 71), 0)
    rotated_key_rows = draw_rotated_key_rows(jax.random.fold_in(key_list[6], 71), 0)
    value_head_rows = noise(key_list[2], (SEQUENCE_TOKENS, KEY_VALUE_HEADS * HEAD_SIZE), 4.0, 24.0, ((0, 16), (1, 2)))
    stride_offset = with_ends(jax.random.randint(key_list[3], (HQ,), 0, STRIDE), jax.random.fold_in(key_list[3], 1), 0, STRIDE - 1).astype(jnp.int32)
    w_out = noise(key_list[4], (HQ * HEAD_SIZE, D), (HQ * HEAD_SIZE) ** -0.5, 0.25, ((0, 2),))
    grad_out = noise_with(key_list[5], (SEQUENCE_TOKENS, D), 1.0, 6.0, ((0, 16), (1, 2)), (0, 1, 16, 2.0))
    return dict(queries=queries, rotated_key_rows=rotated_key_rows, value_head_rows=value_head_rows, stride_offset=stride_offset, w_out=w_out, grad_out=grad_out)


def contract_rows(form, left, right):
    return jnp.einsum(form, left, right, precision=lax.Precision.HIGHEST)


def to_low(values):
    return lax.optimization_barrier(values.astype(jnp.bfloat16)).astype(jnp.float32)


def band_allowed(shard_id, phase_list):
    tokens_q = shard_id * TOKENS_PER_INDEX + jnp.arange(TOKENS_PER_INDEX, dtype=jnp.int32)
    tokens_k = (shard_id - 2) * TOKENS_PER_INDEX + jnp.arange(3 * TOKENS_PER_INDEX, dtype=jnp.int32)
    block_q = tokens_q // BLOCK_TOKENS
    block_k = tokens_k // BLOCK_TOKENS
    causal = (tokens_k[None, :] >= 0) & (tokens_k[None, :] <= tokens_q[:, None])
    nearby = (block_q[:, None] - block_k[None, :]) < LOCAL
    on_stride = ((block_k[None, None, :] + phase_list[:, :, None]) % STRIDE) == STRIDE - 1
    return causal[None, None] & (nearby[None, None] | on_stride[:, :, None, :])


def pick_rows(source, select_mask):
    grouped = source.reshape(-1, STRIDE, BLOCK_TOKENS, source.shape[1], HEAD_SIZE)
    chosen = contract_rows('grs,nsbgd->grnbd', select_mask, grouped)
    return chosen.reshape(chosen.shape[0], chosen.shape[1], -1, HEAD_SIZE)


def reference(queries, rotated_key_rows, value_head_rows, stride_offset, w_out, grad_out):
    scaling = HEAD_SIZE ** -0.5
    phase_list = stride_offset.reshape(KEY_VALUE_HEADS, QUERY_PER_KEY)
    select_mask = (jnp.arange(STRIDE, dtype=jnp.int32)[None, None, :] == (STRIDE - 1 - phase_list)[:, :, None]).astype(jnp.float32)
    query_all_rows = queries.astype(jnp.float32).reshape(SEQUENCE_TOKENS, KEY_VALUE_HEADS, QUERY_PER_KEY, HEAD_SIZE)
    key_all_rows = rotated_key_rows.astype(jnp.float32).reshape(SEQUENCE_TOKENS, KEY_VALUE_HEADS, HEAD_SIZE)
    value_all_rows = value_head_rows.astype(jnp.float32).reshape(SEQUENCE_TOKENS, KEY_VALUE_HEADS, HEAD_SIZE)
    filler_value = jnp.zeros((2 * TOKENS_PER_INDEX, KEY_VALUE_HEADS, HEAD_SIZE), jnp.float32)
    padded_k = jnp.concatenate([filler_value, key_all_rows], axis=0)
    padded_v = jnp.concatenate([filler_value, value_all_rows], axis=0)
    picked_k = pick_rows(key_all_rows, select_mask)
    picked_v = pick_rows(value_all_rows, select_mask)
    picked_rows = TOKENS_PER_INDEX // STRIDE
    picked_count = picked_rows * N_CTX
    tile_rows = BLOCK_TOKENS * math.gcd(picked_count // BLOCK_TOKENS, max(1, 512 // BLOCK_TOKENS))
    tile_count = picked_count // tile_rows

    def shard_inputs(shard_id):
        q_t = lax.dynamic_slice_in_dim(query_all_rows, shard_id * TOKENS_PER_INDEX, TOKENS_PER_INDEX, 0)
        near_k = lax.dynamic_slice_in_dim(padded_k, shard_id * TOKENS_PER_INDEX, 3 * TOKENS_PER_INDEX, 0)
        near_v = lax.dynamic_slice_in_dim(padded_v, shard_id * TOKENS_PER_INDEX, 3 * TOKENS_PER_INDEX, 0)
        return q_t, near_k, near_v, band_allowed(shard_id, phase_list), (shard_id - 2) * picked_rows

    def keep_state(running):
        return running

    def forward_shard(shard_id):
        q_t, near_k, near_v, allowed, bound_rows = shard_inputs(shard_id)
        scores = jnp.where(allowed, contract_rows('tgrd,ugd->grtu', q_t, near_k) * scaling, -jnp.inf)
        row_max = jnp.max(scores, axis=-1)
        weights = jnp.where(allowed, jnp.exp(scores - row_max[..., None]), 0.0)
        row_sum = jnp.sum(weights, axis=-1)
        weighted = contract_rows('grtu,ugd->grtd', to_low(weights), near_v)

        def tile_step(tile_index, running):
            tile_start = tile_index * tile_rows

            def update(running):
                row_max, row_sum, weighted = running
                tile_k = lax.dynamic_slice_in_dim(picked_k, tile_start, tile_rows, 2)
                tile_v = lax.dynamic_slice_in_dim(picked_v, tile_start, tile_rows, 2)
                usable = (tile_start + jnp.arange(tile_rows, dtype=jnp.int32)) < bound_rows
                scores = jnp.where(usable, contract_rows('tgrd,grkd->grtk', q_t, tile_k) * scaling, -jnp.inf)
                new_max = jnp.maximum(row_max, jnp.max(scores, axis=-1))
                weights = jnp.where(usable, jnp.exp(scores - new_max[..., None]), 0.0)
                factor = jnp.exp(row_max - new_max)
                row_sum = row_sum * factor + jnp.sum(weights, axis=-1)
                weighted = weighted * factor[..., None] + contract_rows('grtk,grkd->grtd', to_low(weights), tile_v)
                return new_max, row_sum, weighted

            return lax.cond(tile_start < bound_rows, update, keep_state, running)

        row_max, row_sum, weighted = lax.fori_loop(0, tile_count, tile_step, (row_max, row_sum, weighted))
        mixed = weighted / row_sum[..., None]
        return jnp.transpose(mixed, (2, 0, 1, 3)).astype(jnp.bfloat16), row_max + jnp.log(row_sum)

    shard_outs, shard_logs = lax.map(forward_shard, jnp.arange(N_CTX, dtype=jnp.int32))
    attended_rows = shard_outs.reshape(SEQUENCE_TOKENS, HQ * HEAD_SIZE)
    width_group = HQ * HEAD_SIZE // N_HEAD
    heads_sum = jnp.zeros((SEQUENCE_TOKENS, D), jnp.float32)
    for group_id in range(N_HEAD):
        head_term = jnp.dot(attended_rows[:, group_id * width_group:(group_id + 1) * width_group], w_out[group_id * width_group:(group_id + 1) * width_group], preferred_element_type=jnp.float32)
        heads_sum = heads_sum + to_low(head_term)
    layer_out = heads_sum.astype(jnp.bfloat16)
    grad_w_out = jnp.dot(attended_rows.T, grad_out, preferred_element_type=jnp.float32).astype(jnp.bfloat16)
    attention_gradient = jnp.dot(grad_out, w_out.T, preferred_element_type=jnp.float32).astype(jnp.bfloat16)
    output_gradient_all = attention_gradient.astype(jnp.float32).reshape(SEQUENCE_TOKENS, KEY_VALUE_HEADS, QUERY_PER_KEY, HEAD_SIZE)
    output_all_rows = attended_rows.astype(jnp.float32).reshape(SEQUENCE_TOKENS, KEY_VALUE_HEADS, QUERY_PER_KEY, HEAD_SIZE)

    def backward_shard(running, shard_id):
        key_accumulator, value_accumulator = running
        q_t, near_k, near_v, allowed, bound_rows = shard_inputs(shard_id)
        do_t = lax.dynamic_slice_in_dim(output_gradient_all, shard_id * TOKENS_PER_INDEX, TOKENS_PER_INDEX, 0)
        o_t = lax.dynamic_slice_in_dim(output_all_rows, shard_id * TOKENS_PER_INDEX, TOKENS_PER_INDEX, 0)
        log_t = shard_logs[shard_id]
        row_dot = jnp.transpose(jnp.sum(do_t * o_t, axis=-1), (1, 2, 0))
        scores = contract_rows('tgrd,ugd->grtu', q_t, near_k) * scaling
        weights = jnp.where(allowed, jnp.exp(scores - log_t[..., None]), 0.0)
        grad_near_v = contract_rows('grtu,tgrd->ugd', to_low(weights), do_t)
        grad_weights = contract_rows('tgrd,ugd->grtu', do_t, near_v)
        grad_scores = to_low(weights * (grad_weights - row_dot[..., None]))
        grad_q = contract_rows('grtu,ugd->tgrd', grad_scores, near_k) * scaling
        grad_near_k = contract_rows('grtu,tgrd->ugd', grad_scores, q_t) * scaling

        def tile_step(tile_index, inner):
            tile_start = tile_index * tile_rows

            def update(inner):
                grad_q, grad_pk, grad_pv = inner
                tile_k = lax.dynamic_slice_in_dim(picked_k, tile_start, tile_rows, 2)
                tile_v = lax.dynamic_slice_in_dim(picked_v, tile_start, tile_rows, 2)
                usable = (tile_start + jnp.arange(tile_rows, dtype=jnp.int32)) < bound_rows
                scores = contract_rows('tgrd,grkd->grtk', q_t, tile_k) * scaling
                weights = jnp.where(usable, jnp.exp(scores - log_t[..., None]), 0.0)
                tile_gv = contract_rows('grtk,tgrd->grkd', to_low(weights), do_t)
                grad_weights = contract_rows('tgrd,grkd->grtk', do_t, tile_v)
                grad_scores = to_low(weights * (grad_weights - row_dot[..., None]))
                grad_q = grad_q + contract_rows('grtk,grkd->tgrd', grad_scores, tile_k) * scaling
                tile_gk = contract_rows('grtk,tgrd->grkd', grad_scores, q_t) * scaling
                grad_pk = lax.dynamic_update_slice_in_dim(grad_pk, tile_gk, tile_start, 2)
                grad_pv = lax.dynamic_update_slice_in_dim(grad_pv, tile_gv, tile_start, 2)
                return grad_q, grad_pk, grad_pv

            return lax.cond(tile_start < bound_rows, update, keep_state, inner)

        empty_state = jnp.zeros((KEY_VALUE_HEADS, QUERY_PER_KEY, picked_count, HEAD_SIZE), jnp.float32)
        grad_q, grad_pk, grad_pv = lax.fori_loop(0, tile_count, tile_step, (grad_q, empty_state, empty_state))

        def place(picked_gradient, grad_near):
            spread_row_list = contract_rows('xij,xiucz->ujcxz', select_mask, picked_gradient.reshape(KEY_VALUE_HEADS, QUERY_PER_KEY, -1, BLOCK_TOKENS, HEAD_SIZE)).reshape(SEQUENCE_TOKENS, KEY_VALUE_HEADS, HEAD_SIZE)
            padded = jnp.concatenate([filler_value, spread_row_list], axis=0)
            region = lax.dynamic_slice_in_dim(padded, shard_id * TOKENS_PER_INDEX, 3 * TOKENS_PER_INDEX, 0) + grad_near
            padded = lax.dynamic_update_slice_in_dim(padded, region, shard_id * TOKENS_PER_INDEX, 0)
            return to_low(padded[2 * TOKENS_PER_INDEX:])

        key_accumulator = key_accumulator + place(grad_pk, grad_near_k)
        value_accumulator = value_accumulator + place(grad_pv, grad_near_v)
        return (key_accumulator, value_accumulator), grad_q.astype(jnp.bfloat16)

    initial_accumulator = jnp.zeros((SEQUENCE_TOKENS, KEY_VALUE_HEADS, HEAD_SIZE), jnp.float32)
    (key_accumulator, value_accumulator), grad_shards = lax.scan(backward_shard, (initial_accumulator, initial_accumulator), jnp.arange(N_CTX, dtype=jnp.int32))
    grad_queries = grad_shards.reshape(SEQUENCE_TOKENS, HQ * HEAD_SIZE)
    key_gradient = key_accumulator.astype(jnp.bfloat16).reshape(SEQUENCE_TOKENS, KEY_VALUE_HEADS * HEAD_SIZE)
    value_gradient = value_accumulator.astype(jnp.bfloat16).reshape(SEQUENCE_TOKENS, KEY_VALUE_HEADS * HEAD_SIZE)
    return (layer_out, grad_queries, key_gradient, value_gradient, grad_w_out)
```

```python
import functools
import math

import jax
import jax.numpy as jnp
from jax import lax
from jax.experimental import pallas as pl
from jax.experimental.pallas import tpu as pltpu
from jax.sharding import PartitionSpec as P

HEAD_SIZE = 128
BLOCK_TOKENS = 64
LOCAL = 16
STRIDE = 8
TILE = 128
BF16 = jnp.bfloat16
F32 = jnp.float32
SCALE = HEAD_SIZE ** (-0.5)
EXP2_SCALE = SCALE * math.log2(math.e)
MASKED = -1e30

VMEM = pl.BlockSpec(memory_space=pltpu.VMEM)
SMEM = pl.BlockSpec(memory_space=pltpu.SMEM)
NN = (((1,), (0,)), ((), ()))
NT = (((1,), (1,)), ((), ()))
TN = (((0,), (0,)), ((), ()))


def mm(left, right, dims=NN):
    return lax.dot_general(left, right, dims, preferred_element_type=F32)


def call(kernel, name, ins, out_shapes, scratch=(), mib=32, flops=0):
    nbytes = sum(a.size * a.dtype.itemsize for a in ins)
    nbytes += sum(math.prod(s.shape) * s.dtype.itemsize for s in out_shapes)
    return pl.pallas_call(
        kernel,
        name=name,
        out_shape=out_shapes,
        in_specs=[SMEM if a.dtype == jnp.int32 else VMEM for a in ins],
        out_specs=[VMEM] * len(out_shapes),
        scratch_shapes=list(scratch),
        compiler_params=pltpu.CompilerParams(vmem_limit_bytes=mib * 2**20),
        cost_estimate=pl.CostEstimate(flops=flops, bytes_accessed=nbytes, transcendentals=0),
    )(*ins)


def shape(dims, dtype):
    return jax.ShapeDtypeStruct(dims, dtype)


def flips(count, bit):
    return [(i, i ^ bit) for i in range(count)]


def slot_owner(ctx, slot, order):
    mask = 0
    for k, bit in enumerate(order):
        if slot >> k & 1:
            mask |= bit
    return ctx ^ mask


def pack_kernel(phase_ref, k_ref, v_ref, kv_ref, pick_ref):
    rows = k_ref.shape[0]
    kv_ref[:rows] = k_ref[...]
    kv_ref[rows:] = v_ref[...]
    for r in range(2):
        start = pl.multiple_of((STRIDE - 1 - phase_ref[r]) * BLOCK_TOKENS, BLOCK_TOKENS)
        at = 2 * r * BLOCK_TOKENS
        pick_ref[at : at + BLOCK_TOKENS] = k_ref[pl.ds(start, BLOCK_TOKENS)]
        pick_ref[at + BLOCK_TOKENS : at + 2 * BLOCK_TOKENS] = v_ref[pl.ds(start, BLOCK_TOKENS)]


def load_window(core, own_ref, core_ref, two_ref, two_core_ref, part, out):
    rows = own_ref.shape[0] // 2
    piece = pl.ds(part * rows, rows)
    out[:rows] = two_ref[piece]
    out[rows : 2 * rows] = jnp.where(core == 0, two_core_ref[piece], core_ref[piece])
    out[2 * rows :] = own_ref[piece]


def band_scores(ctx, tile, chunk, tiles, k_win, q_tile):
    start = (tile + chunk) * TILE
    s = mm(k_win[start : start + TILE], q_tile, NT)
    if chunk == 0 or chunk == 2 * tiles:
        key = lax.broadcasted_iota(jnp.int32, s.shape, 0)
        token = lax.broadcasted_iota(jnp.int32, s.shape, 1) % TILE
        if chunk == 0:
            s = jnp.where(key // BLOCK_TOKENS > token // BLOCK_TOKENS, s, MASKED)
        else:
            s = jnp.where(key <= token, s, MASKED)
    if tile + chunk < 2 * tiles:
        first = 2 - (tile + chunk) // tiles
        s = jnp.where(ctx >= first, s, MASKED)
    return s


def both_heads(ref, tile):
    rows = slice(tile * TILE, (tile + 1) * TILE)
    return jnp.concatenate([ref[rows, :HEAD_SIZE], ref[rows, HEAD_SIZE:]], axis=0)


def band_forward_kernel(q_ref, own_ref, core_ref, two_ref, two_core_ref, out_ref, max_ref, sum_ref, k_win, v_win, s_buf, p_buf):
    ctx = lax.axis_index("ctx")
    core = ctx % 2
    tiles = q_ref.shape[0] // TILE
    chunks = 2 * tiles + 1
    load_window(core, own_ref, core_ref, two_ref, two_core_ref, 0, k_win)
    load_window(core, own_ref, core_ref, two_ref, two_core_ref, 1, v_win)
    for tile in range(tiles):
        q_tile = both_heads(q_ref, tile)
        top = None
        for chunk in range(chunks):
            s = band_scores(ctx, tile, chunk, tiles, k_win, q_tile)
            s_buf[chunk * TILE : (chunk + 1) * TILE] = s
            here = jnp.max(s.reshape(TILE // 8, 8, 2 * TILE), axis=0)
            top = here if top is None else jnp.maximum(top, here)
        top = jnp.max(top, axis=0, keepdims=True)
        total = None
        for chunk in range(chunks):
            p = jnp.exp2((s_buf[chunk * TILE : (chunk + 1) * TILE] - top) * EXP2_SCALE)
            here = jnp.sum(p.reshape(TILE // 8, 8, 2 * TILE), axis=0)
            total = here if total is None else total + here
            p_buf[chunk * TILE : (chunk + 1) * TILE] = p.astype(BF16)
        total = jnp.sum(total, axis=0, keepdims=True)
        out = mm(v_win[tile * TILE : (tile + chunks) * TILE], p_buf[...], TN)
        at = slice(tile * TILE, (tile + 1) * TILE)
        for r in range(2):
            half = slice(r * TILE, (r + 1) * TILE)
            out_ref[r, :, at] = out[:, half]
            max_ref[r : r + 1, at] = top[:, half]
            sum_ref[r : r + 1, at] = total[:, half]


def band_backward_kernel(
    q_ref, do_ref, own_ref, core_ref, two_ref, two_core_ref, lse_ref, dot_ref, dq_in_ref,
    dq_ref, own_out, one_out, two_out, k_win, v_win, dk_acc, dv_acc, p_buf, ds_buf,
):
    ctx = lax.axis_index("ctx")
    core = ctx % 2
    rows = q_ref.shape[0]
    tiles = rows // TILE
    chunks = 2 * tiles + 1
    load_window(core, own_ref, core_ref, two_ref, two_core_ref, 0, k_win)
    load_window(core, own_ref, core_ref, two_ref, two_core_ref, 1, v_win)
    dk_acc[...] = jnp.zeros_like(dk_acc)
    dv_acc[...] = jnp.zeros_like(dv_acc)
    for tile in range(tiles):
        q_tile = both_heads(q_ref, tile)
        do_tile = both_heads(do_ref, tile)
        at = slice(tile * TILE, (tile + 1) * TILE)
        lse = jnp.concatenate([lse_ref[0:1, at], lse_ref[1:2, at]], axis=1)
        dot = jnp.concatenate([dot_ref[0:1, at], dot_ref[1:2, at]], axis=1)
        for chunk in range(chunks):
            s = band_scores(ctx, tile, chunk, tiles, k_win, q_tile)
            p = jnp.exp2((s - lse) * EXP2_SCALE)
            start = (tile + chunk) * TILE
            dp = mm(v_win[start : start + TILE], do_tile, NT)
            piece = slice(chunk * TILE, (chunk + 1) * TILE)
            p_buf[piece] = p.astype(BF16)
            ds_buf[piece] = (p * (dp - dot)).astype(BF16)
        window = slice(tile * TILE, (tile + chunks) * TILE)
        dv_acc[window] += mm(p_buf[...], do_tile)
        dk_acc[window] += mm(ds_buf[...], q_tile)
        dq = mm(k_win[window], ds_buf[...], TN)
        for r in range(2):
            whole = (dq[:, r * TILE : (r + 1) * TILE] + dq_in_ref[r, :, at]) * SCALE
            dq_ref[at, r * HEAD_SIZE : (r + 1) * HEAD_SIZE] = whole.T.astype(BF16)
    for index, out in ((0, two_out), (1, one_out), (2, own_out)):
        part = slice(index * rows, (index + 1) * rows)
        out[:rows] = (dk_acc[part] * SCALE).astype(BF16)
        out[rows:] = dv_acc[part].astype(BF16)


def load_picked(mine_ref, other_ref, r, part, out):
    size = 4 * BLOCK_TOKENS
    slots = mine_ref.shape[0] // size
    for slot in range(2 * slots):
        source = mine_ref if slot < slots else other_ref
        start = (slot % slots) * size + (2 * r + part) * BLOCK_TOKENS
        out[slot * BLOCK_TOKENS : (slot + 1) * BLOCK_TOKENS] = source[start : start + BLOCK_TOKENS]


def slot_scores(ctx, slot, order, phase, token_start, s):
    owner = slot_owner(ctx, slot, order)
    token = token_start + lax.broadcasted_iota(jnp.int32, s.shape, 1)
    first = jnp.where(owner < ctx - 2, 0, jnp.where(owner == ctx - 2, (STRIDE - 1 - phase) * BLOCK_TOKENS, 2**30))
    return jnp.where(token >= first, s, MASKED)


def stride_forward_kernel(order, phase_ref, q_ref, mine_ref, other_ref, out_in_ref, max_in_ref, sum_in_ref, att_ref, lse_ref, k_pick, v_pick, s_buf, p_buf):
    ctx = lax.axis_index("ctx")
    rows = q_ref.shape[0]
    slots = k_pick.shape[0] // BLOCK_TOKENS
    width = 2 * TILE
    for r in range(2):
        load_picked(mine_ref, other_ref, r, 0, k_pick)
        load_picked(mine_ref, other_ref, r, 1, v_pick)
        for token_start in range(0, rows, width):
            at = slice(token_start, token_start + width)
            q_tile = q_ref[at, r * HEAD_SIZE : (r + 1) * HEAD_SIZE]
            old = max_in_ref[r : r + 1, at]
            top = None
            for slot in range(slots):
                piece = slice(slot * BLOCK_TOKENS, (slot + 1) * BLOCK_TOKENS)
                s = slot_scores(ctx, slot, order, phase_ref[r], token_start, mm(k_pick[piece], q_tile, NT))
                s_buf[piece] = s
                here = jnp.max(s.reshape(BLOCK_TOKENS // 8, 8, width), axis=0)
                top = here if top is None else jnp.maximum(top, here)
            top = jnp.maximum(jnp.max(top, axis=0, keepdims=True), old)
            total = None
            for slot in range(slots):
                piece = slice(slot * BLOCK_TOKENS, (slot + 1) * BLOCK_TOKENS)
                p = jnp.exp2((s_buf[piece] - top) * EXP2_SCALE)
                here = jnp.sum(p.reshape(BLOCK_TOKENS // 8, 8, width), axis=0)
                total = here if total is None else total + here
                p_buf[piece] = p.astype(BF16)
            factor = jnp.exp2((old - top) * EXP2_SCALE)
            total = jnp.sum(total, axis=0, keepdims=True) + sum_in_ref[r : r + 1, at] * factor
            out = mm(v_pick[...], p_buf[...], TN) + out_in_ref[r, :, at] * factor
            out = out / total
            att_ref[at, r * HEAD_SIZE : (r + 1) * HEAD_SIZE] = out.T.astype(BF16)
            lse_ref[r : r + 1, at] = top + jnp.log2(total) * (1.0 / EXP2_SCALE)


def stride_backward_kernel(order, phase_ref, q_ref, grad_own_ref, grad_got_ref, att_ref, lse_ref, mine_ref, other_ref, do_ref, dot_ref, dq_ref, keep_ref, send_ref, k_pick, v_pick, p_buf, ds_buf):
    ctx = lax.axis_index("ctx")
    rows = q_ref.shape[0]
    slots = k_pick.shape[0] // BLOCK_TOKENS
    width = 2 * TILE
    size = 4 * BLOCK_TOKENS
    do_ref[...] = (grad_own_ref[...] + grad_got_ref[...].astype(F32)).astype(BF16)
    for r in range(2):
        head = slice(r * HEAD_SIZE, (r + 1) * HEAD_SIZE)
        product = do_ref[:, head].astype(F32) * att_ref[:, head].astype(F32)
        dot_ref[r : r + 1, :] = jnp.sum(product.T, axis=0, keepdims=True)
        load_picked(mine_ref, other_ref, r, 0, k_pick)
        load_picked(mine_ref, other_ref, r, 1, v_pick)
        for token_start in range(0, rows, width):
            at = slice(token_start, token_start + width)
            q_tile = q_ref[at, head]
            do_tile = do_ref[at, head]
            lse = lse_ref[r : r + 1, at]
            dot = dot_ref[r : r + 1, at]
            for slot in range(slots):
                piece = slice(slot * BLOCK_TOKENS, (slot + 1) * BLOCK_TOKENS)
                s = slot_scores(ctx, slot, order, phase_ref[r], token_start, mm(k_pick[piece], q_tile, NT))
                p = jnp.exp2((s - lse) * EXP2_SCALE)
                dp = mm(v_pick[piece], do_tile, NT)
                p_buf[piece, at] = p.astype(BF16)
                ds_buf[piece, at] = (p * (dp - dot)).astype(BF16)
        dv = mm(p_buf[...], do_ref[:, head])
        dk = mm(ds_buf[...], q_ref[:, head]) * SCALE
        dq_ref[r] = mm(k_pick[...], ds_buf[...], TN)
        for slot in range(slots):
            target = keep_ref if slot < slots // 2 else send_ref
            start = (slot % (slots // 2)) * size + 2 * r * BLOCK_TOKENS
            piece = slice(slot * BLOCK_TOKENS, (slot + 1) * BLOCK_TOKENS)
            target[start : start + BLOCK_TOKENS] = dk[piece].astype(BF16)
            target[start + BLOCK_TOKENS : start + 2 * BLOCK_TOKENS] = dv[piece].astype(BF16)


def finish_kernel(phase_ref, own_ref, core_ref, two_ref, stride_a_ref, stride_b_ref, dk_ref, dv_ref, acc):
    even = lax.axis_index("ctx") % 2 == 0
    rows = dk_ref.shape[0]
    acc[...] = own_ref[...].astype(F32) + two_ref[...].astype(F32) + jnp.where(even, core_ref[...].astype(F32), 0.0)
    stride = stride_a_ref[...].astype(F32) + stride_b_ref[...].astype(F32)
    for r in range(2):
        for part in range(2):
            start = pl.multiple_of(part * rows + (STRIDE - 1 - phase_ref[r]) * BLOCK_TOKENS, BLOCK_TOKENS)
            at = (2 * r + part) * BLOCK_TOKENS
            acc[pl.ds(start, BLOCK_TOKENS)] += stride[at : at + BLOCK_TOKENS]
    dk_ref[...] = acc[:rows].astype(BF16)
    dv_ref[...] = acc[rows:].astype(BF16)


def grad_own_kernel(g_ref, w_ref, out_ref):
    width = g_ref.shape[1]
    start = pl.multiple_of(lax.axis_index("head") * width, width)
    out_ref[...] = mm(g_ref[...], w_ref[:, pl.ds(start, width)], NT)


def grad_other_kernel(g_ref, near_ref, far_ref, out_ref):
    core = lax.axis_index("ctx") % 2
    width = near_ref.shape[1]
    near = pl.ds(pl.multiple_of(core * width, width), width)
    far = pl.ds(pl.multiple_of((1 - core) * width, width), width)
    total = mm(g_ref[:, near], near_ref[...], NT) + mm(g_ref[:, far], far_ref[...], NT)
    out_ref[...] = total.astype(BF16)


def layer_out_kernel(own_ref, other_ref, w_ref, near_ref, far_ref, out_ref):
    core = lax.axis_index("ctx") % 2
    width = near_ref.shape[1]
    base = lax.axis_index("head") * 2 * width
    step = 256
    for part, source in ((core, near_ref), (1 - core, far_ref)):
        for at in range(0, width, step):
            start = part * width + at
            w_own = w_ref[:, pl.ds(pl.multiple_of(base + start, step), step)]
            total = mm(own_ref[...], w_own) + mm(other_ref[...], source[:, at : at + step])
            out_ref[:, pl.ds(pl.multiple_of(start, step), step)] = total.astype(BF16)


def weight_grad_kernel(bits, att_ref, g_ref, keep_ref, send_ref):
    ctx = lax.axis_index("ctx")
    _, _, cols = keep_ref.shape
    blocks = 1 << len(bits)
    att = att_ref[...].T
    for slot in range(blocks):
        mask = 0
        for k, bit in enumerate(bits):
            if slot >> (len(bits) - 1 - k) & 1:
                mask |= bit
        block = (ctx % blocks) ^ mask
        term = mm(att, g_ref[:, pl.ds(pl.multiple_of(block * cols, cols), cols)]).astype(BF16)
        if slot < blocks // 2:
            keep_ref[slot] = term
        else:
            send_ref[slot - blocks // 2] = term


def add(left, right):
    return left.astype(F32) + right.astype(F32)


def body(queries, rotated_key_rows, value_head_rows, stride_offset, w_out, grad_out):
    rows = queries.shape[0]
    n_ctx = lax.axis_size("ctx")
    n_head = lax.axis_size("head")
    ctx = lax.axis_index("ctx")
    head = lax.axis_index("head")
    core = ctx % 2
    model = w_out.shape[1]
    width = grad_out.shape[1]
    head_rows = w_out.shape[0]
    ratio = n_ctx // n_head
    cols = model // n_ctx
    flip = functools.partial(flips, n_ctx)
    swap = [(0, 1), (1, 0)]
    scores = rows * 2 * HEAD_SIZE * 2
    proj = 2 * rows * head_rows * width

    kv, picks = call(
        pack_kernel, "pack", [stride_offset, rotated_key_rows, value_head_rows],
        [shape((2 * rows, HEAD_SIZE), BF16), shape((4 * BLOCK_TOKENS, HEAD_SIZE), BF16)],
    )
    if n_head == 2:
        half = width // 2
        piece = lax.dynamic_slice(w_out, (0, (1 - head) * width + core * half), (head_rows, half))
        w_near = lax.ppermute(piece, "head", swap)
        w_far = lax.ppermute(w_near, "ctx", flip(1))
    else:
        w_all = lax.all_to_all(w_out, "head", 1, 0, tiled=True)
    kv_core = lax.ppermute(kv, "ctx", flip(1))
    kv_two = lax.ppermute(kv, "ctx", [(i, i + 2) for i in range(n_ctx - 2)])
    kv_two_core = lax.ppermute(kv_two, "ctx", flip(1))
    order = []
    bit = 4
    while bit < n_ctx:
        order.append(bit)
        bit *= 2
    order += [2, 1]
    for bit in order[:-1]:
        picks = jnp.concatenate([picks, lax.ppermute(picks, "ctx", flip(bit))], axis=0)
    picks_other = lax.ppermute(picks, "ctx", flip(1))

    chunk_rows = (2 * (rows // TILE) + 1) * TILE
    window = pltpu.VMEM((3 * rows, HEAD_SIZE), BF16)
    out, top, total = call(
        band_forward_kernel, "band_forward", [queries, kv, kv_core, kv_two, kv_two_core],
        [shape((2, HEAD_SIZE, rows), F32), shape((2, rows), F32), shape((2, rows), F32)],
        [window, window, pltpu.VMEM((chunk_rows, 2 * TILE), F32), pltpu.VMEM((chunk_rows, 2 * TILE), BF16)],
        flops=2 * scores * chunk_rows,
    )
    if n_head == 2:
        grad_own, = call(
            grad_own_kernel, "grad_own", [grad_out, w_out], [shape((rows, head_rows), F32)], flops=proj
        )
        grad_other, = call(
            grad_other_kernel, "grad_other", [grad_out, w_near, w_far],
            [shape((rows, head_rows), BF16)], flops=proj,
        )
        grad_got = lax.ppermute(grad_other, "head", swap)
    else:
        grad_all = mm(grad_out, w_all, NT).astype(BF16)
        grad_all = lax.all_to_all(grad_all.reshape(rows, n_head, head_rows), "head", 1, 0, tiled=True)
        grad_all = grad_all.reshape(n_head, rows, head_rows).astype(F32)
        grad_own = jnp.sum(grad_all, axis=0)
        grad_got = jnp.zeros((rows, head_rows), BF16)
    picked_rows = n_ctx * BLOCK_TOKENS
    pick = pltpu.VMEM((picked_rows, HEAD_SIZE), BF16)
    attended, lse = call(
        functools.partial(stride_forward_kernel, tuple(order)), "stride_forward",
        [stride_offset, queries, picks, picks_other, out, top, total],
        [shape((rows, head_rows), BF16), shape((2, rows), F32)],
        [pick, pick, pltpu.VMEM((picked_rows, 2 * TILE), F32), pltpu.VMEM((picked_rows, 2 * TILE), BF16)],
        flops=2 * scores * picked_rows,
    )
    if n_head == 2:
        att_other = lax.ppermute(attended, "head", swap)
    grad_att, row_dot, grad_q, stride_keep, stride_send = call(
        functools.partial(stride_backward_kernel, tuple(order)), "stride_backward",
        [stride_offset, queries, grad_own, grad_got, attended, lse, picks, picks_other],
        [
            shape((rows, head_rows), BF16), shape((2, rows), F32), shape((2, HEAD_SIZE, rows), F32),
            shape(picks.shape, BF16), shape(picks.shape, BF16),
        ],
        [pick, pick, pltpu.VMEM((picked_rows, rows), BF16), pltpu.VMEM((picked_rows, rows), BF16)],
        flops=5 * scores * picked_rows,
    )
    for bit in reversed(order):
        got = lax.ppermute(stride_send, "ctx", flip(bit))
        if bit != order[0]:
            both = add(stride_keep, got)
            middle = both.shape[0] // 2
            stride_keep, stride_send = both[:middle], both[middle:].astype(BF16)
    stride_got = got

    grad_queries, own, one, two = call(
        band_backward_kernel, "band_backward",
        [queries, grad_att, kv, kv_core, kv_two, kv_two_core, lse, row_dot, grad_q],
        [shape((rows, head_rows), BF16)] + [shape((2 * rows, HEAD_SIZE), BF16)] * 3,
        [
            window, window, pltpu.VMEM((3 * rows, HEAD_SIZE), F32), pltpu.VMEM((3 * rows, HEAD_SIZE), F32),
            pltpu.VMEM((chunk_rows, 2 * TILE), BF16), pltpu.VMEM((chunk_rows, 2 * TILE), BF16),
        ],
        flops=5 * scores * chunk_rows,
    )
    one_got = lax.ppermute(one, "ctx", flip(1))
    two = jnp.where(core == 1, add(two, one_got), two.astype(F32)).astype(BF16)
    two_got = lax.ppermute(two, "ctx", [(i + 2, i) for i in range(n_ctx - 2)])

    if n_head == 2:
        layer_out, = call(
            layer_out_kernel, "layer_out", [attended, att_other, w_out, w_near, w_far],
            [shape((rows, width), BF16)], flops=2 * proj,
        )
        bits = []
        bit = 1
        while bit < ratio:
            bits.append(bit)
            bit *= 2
        high = n_ctx // 2
        ended = []
        for source, name in ((attended, "weight_grad_own"), (att_other, "weight_grad_other")):
            part = shape((ratio // 2, head_rows, cols), BF16)
            keep, send = call(
                functools.partial(weight_grad_kernel, tuple(bits)), name, [source, grad_out],
                [part, part], flops=proj,
            )
            for bit in bits:
                got = lax.ppermute(send, "ctx", flip(bit))
                both = add(keep, got)
                if bit != bits[-1]:
                    middle = both.shape[0] // 2
                    keep, send = both[:middle], both[middle:].astype(BF16)
            ended.append(both[0])
        sum_own, sum_other = ended
        same = (ctx // high) == head
        first_route, second_route = [], []
        for c in range(n_ctx):
            for h in range(2):
                here = 2 * c + h
                if c // high == h:
                    first_route.append((here, 2 * c + 1 - h))
                else:
                    first_route.append((here, 2 * (c ^ high) + h))
                    second_route.append((here, 2 * (c ^ high) + 1 - h))
        other_low = sum_other.astype(BF16)
        first = lax.ppermute(jnp.where(same, other_low, sum_own.astype(BF16)), ("ctx", "head"), first_route)
        second = lax.ppermute(other_low, ("ctx", "head"), second_route)
        grad_w_out = (first.astype(F32) + jnp.where(same, sum_own, second.astype(F32))).astype(BF16)
    else:
        att_all = lax.all_gather(attended, "head", axis=1, tiled=True)
        layer_out = mm(att_all, w_all).astype(BF16)
        terms = mm(att_all, grad_out, TN).astype(BF16).reshape(n_head, head_rows, ratio, cols)
        terms = jnp.transpose(terms, (0, 2, 1, 3)).reshape(n_ctx, head_rows, cols)
        terms = lax.psum_scatter(terms, "ctx", scatter_dimension=0, tiled=True)[0]
        route = []
        for c in range(n_ctx):
            for h in range(n_head):
                target = (h * ratio + c % ratio) * n_head + c // ratio
                route.append((c * n_head + h, target))
        grad_w_out = lax.ppermute(terms, ("ctx", "head"), route)

    key_gradient, value_gradient = call(
        finish_kernel, "finish", [stride_offset, own, one_got, two_got, stride_keep, stride_got],
        [shape((rows, HEAD_SIZE), BF16)] * 2,
        [pltpu.VMEM((2 * rows, HEAD_SIZE), F32)],
    )
    return (layer_out, grad_queries, key_gradient, value_gradient, grad_w_out)


def solution(mesh):
    placed = (
        P("ctx", "head"),
        P("ctx", "head"),
        P("ctx", "head"),
        P("head"),
        P("head", None),
        P("ctx", "head"),
    )
    return jax.shard_map(
        body,
        mesh=mesh,
        in_specs=placed,
        out_specs=(
            P("ctx", "head"),
            P("ctx", "head"),
            P("ctx", "head"),
            P("ctx", "head"),
            P("head", "ctx"),
        ),
        check_vma=False,
    )
```

```python
import functools
import math

import jax
import jax.numpy as jnp
from jax import lax
from jax.experimental import pallas as pl
from jax.experimental.pallas import tpu as pltpu
from jax.sharding import PartitionSpec as P

HEAD_SIZE = 128
BLOCK_TOKENS = 64
LOCAL = 16
STRIDE = 8
TILE = 128
BF16 = jnp.bfloat16
F32 = jnp.float32
SCALE = HEAD_SIZE ** (-0.5)
EXP2_SCALE = SCALE * math.log2(math.e)
MASKED = -1e30

VMEM = pl.BlockSpec(memory_space=pltpu.VMEM)
ANY = pl.BlockSpec(memory_space=pl.ANY)
HBM = pl.BlockSpec(memory_space=pltpu.HBM)
SMEM = pl.BlockSpec(memory_space=pltpu.SMEM)
NN = (((1,), (0,)), ((), ()))
NT = (((1,), (1,)), ((), ()))
TN = (((0,), (0,)), ((), ()))


def mm(left, right, dims=NN):
    return lax.dot_general(left, right, dims, preferred_element_type=F32)


USEC = {'pack': 2, 'grad_own': 2, 'grad_other': 0.1, 'band_forward': 0.1, 'stride_forward': 36, 'stride_backward': 46, 'band_backward': 40, 'layer_out': 26, 'finish': 15, 'last_sum': 7, 'weight_grad_own': 8, 'weight_grad_other': 8}


class Sequence:
    def __init__(self):
        self.last = []

    def __call__(self, kernel, name, ins, out_shapes, scratch=(), mib=32, flops=0, after=(), far=(), out_space=VMEM):
        extra = self.last + list(after)
        count = len(ins)

        def wrapped(*refs):
            rest = refs[count + len(extra) :]
            kernel(*refs[:count], *rest[: len(out_shapes)], *rest[len(out_shapes) + 1 :])
            token = rest[len(out_shapes)]
            token[...] = jnp.zeros_like(token)

        specs = [SMEM if a.dtype == jnp.int32 else VMEM for a in ins]
        for index in far:
            specs[index] = HBM
        outs = pl.pallas_call(
            wrapped,
            name=name,
            out_shape=list(out_shapes) + [shape((8, 128), F32)],
            in_specs=specs + [ANY] * len(extra),
            out_specs=[out_space] * len(out_shapes) + [VMEM],
            scratch_shapes=list(scratch),
            compiler_params=pltpu.CompilerParams(vmem_limit_bytes=mib * 2**20),
            cost_estimate=pl.CostEstimate(flops=int(1e9 * USEC.get(name, 0.1)), bytes_accessed=1, transcendentals=0),
        )(*ins, *extra)
        self.last = [outs[-1]]
        return outs[:-1]


    def hold(self, array, after=()):
        extra = self.last + list(after)

        def kernel(*refs):
            token = refs[-1]
            token[...] = jnp.zeros_like(token)

        held, token = pl.pallas_call(
            kernel,
            name="hold",
            out_shape=[shape(array.shape, array.dtype), shape((8, 128), F32)],
            in_specs=[ANY] * (1 + len(extra)),
            out_specs=[ANY, VMEM],
            input_output_aliases={0: 0},
            compiler_params=pltpu.CompilerParams(vmem_limit_bytes=2**20),
            cost_estimate=pl.CostEstimate(flops=1, bytes_accessed=1, transcendentals=0),
        )(array, *extra)
        self.last = [token]
        return held


def shape(dims, dtype):
    return jax.ShapeDtypeStruct(dims, dtype)


def flips(count, bit):
    return [(i, i ^ bit) for i in range(count)]


def slot_owner(ctx, slot, order):
    mask = 0
    for k, bit in enumerate(order):
        if slot >> k & 1:
            mask |= bit
    return ctx ^ mask


def run_copies(pairs, sem):
    copies = [pltpu.make_async_copy(src, dst, sem.at[i]) for i, (src, dst) in enumerate(pairs)]
    for copy in copies:
        copy.start()
    return copies


def pack_kernel(phase_ref, k_ref, v_ref, *refs):
    if len(refs) == 5:
        kv_ref, pick_ref, kv_buf, in_sem, out_sem = refs
        inward = []
    else:
        w_ref, kv_ref, pick_ref, piece_ref, kv_buf, piece_buf, in_sem, out_sem = refs
        cols = piece_ref.shape[1]
        start = (1 - lax.axis_index("head")) * 2 * cols + lax.axis_index("ctx") % 2 * cols
        inward = [(w_ref.at[:, pl.ds(pl.multiple_of(start, cols), cols)], piece_buf)]
    rows = k_ref.shape[0]
    inward = [(k_ref, kv_buf.at[pl.ds(0, rows)]), (v_ref, kv_buf.at[pl.ds(rows, rows)])] + inward
    outward = []
    for r in range(2):
        for part in range(2):
            start = pl.multiple_of(part * rows + (STRIDE - 1 - phase_ref[r]) * BLOCK_TOKENS, BLOCK_TOKENS)
            at = (2 * r + part) * BLOCK_TOKENS
            outward.append((kv_buf.at[pl.ds(start, BLOCK_TOKENS)], pick_ref.at[pl.ds(at, BLOCK_TOKENS)]))
    outward.append((kv_buf, kv_ref))
    coming = run_copies(inward, in_sem)
    coming[0].wait()
    coming[1].wait()
    going = run_copies(outward, out_sem)
    for copy in coming[2:]:
        copy.wait()
        last = pltpu.make_async_copy(piece_buf, piece_ref, out_sem.at[len(outward)])
        last.start()
        going.append(last)
    for copy in going:
        copy.wait()


def join_kernel(first_ref, second_ref, out_ref):
    middle = first_ref.shape[0]
    out_ref[:middle] = first_ref[...]
    out_ref[middle:] = second_ref[...]


def join(run, name, first, second, after=()):
    return run(join_kernel, name, [first, second], [shape((2 * first.shape[0],) + first.shape[1:], BF16)], after=after)[0]


def load_window(core, own_ref, core_ref, two_ref, two_core_ref, part, out):
    rows = own_ref.shape[0] // 2
    piece = pl.ds(part * rows, rows)
    out[:rows] = two_ref[piece]
    out[rows : 2 * rows] = jnp.where(core == 0, two_core_ref[piece], core_ref[piece])
    out[2 * rows :] = own_ref[piece]


def band_scores(ctx, tile, chunk, tiles, k_win, q_tile):
    start = (tile + chunk) * TILE
    s = mm(k_win[start : start + TILE], q_tile, NT)
    if chunk == 0 or chunk == 2 * tiles:
        key = lax.broadcasted_iota(jnp.int32, s.shape, 0)
        token = lax.broadcasted_iota(jnp.int32, s.shape, 1) % TILE
        if chunk == 0:
            s = jnp.where(key // BLOCK_TOKENS > token // BLOCK_TOKENS, s, MASKED)
        else:
            s = jnp.where(key <= token, s, MASKED)
    if tile + chunk < 2 * tiles:
        first = 2 - (tile + chunk) // tiles
        s = jnp.where(ctx >= first, s, MASKED)
    return s


def both_heads(ref, tile):
    rows = slice(tile * TILE, (tile + 1) * TILE)
    return jnp.concatenate([ref[rows, :HEAD_SIZE], ref[rows, HEAD_SIZE:]], axis=0)


def band_forward_kernel(q_ref, own_ref, core_ref, two_ref, two_core_ref, out_ref, max_ref, sum_ref, k_win, v_win, s_buf, p_buf):
    ctx = lax.axis_index("ctx")
    core = ctx % 2
    tiles = q_ref.shape[0] // TILE
    chunks = 2 * tiles + 1
    load_window(core, own_ref, core_ref, two_ref, two_core_ref, 0, k_win)
    load_window(core, own_ref, core_ref, two_ref, two_core_ref, 1, v_win)
    for tile in range(tiles):
        q_tile = both_heads(q_ref, tile)
        top = None
        for chunk in range(chunks):
            s = band_scores(ctx, tile, chunk, tiles, k_win, q_tile)
            s_buf[chunk * TILE : (chunk + 1) * TILE] = s
            here = jnp.max(s.reshape(TILE // 8, 8, 2 * TILE), axis=0)
            top = here if top is None else jnp.maximum(top, here)
        top = jnp.max(top, axis=0, keepdims=True)
        total = None
        for chunk in range(chunks):
            p = jnp.exp2((s_buf[chunk * TILE : (chunk + 1) * TILE] - top) * EXP2_SCALE)
            here = jnp.sum(p.reshape(TILE // 8, 8, 2 * TILE), axis=0)
            total = here if total is None else total + here
            p_buf[chunk * TILE : (chunk + 1) * TILE] = p.astype(BF16)
        total = jnp.sum(total, axis=0, keepdims=True)
        out = mm(v_win[tile * TILE : (tile + chunks) * TILE], p_buf[...], TN)
        at = slice(tile * TILE, (tile + 1) * TILE)
        for r in range(2):
            half = slice(r * TILE, (r + 1) * TILE)
            out_ref[r, :, at] = out[:, half]
            max_ref[r : r + 1, at] = top[:, half]
            sum_ref[r : r + 1, at] = total[:, half]


def band_backward_kernel(
    q_ref, do_ref, own_ref, core_ref, two_ref, two_core_ref, lse_ref, dot_ref, dq_in_ref,
    dq_ref, own_out, one_out, two_out, k_win, v_win, dk_acc, dv_acc, p_buf, ds_buf,
):
    ctx = lax.axis_index("ctx")
    core = ctx % 2
    rows = q_ref.shape[0]
    tiles = rows // TILE
    chunks = 2 * tiles + 1
    load_window(core, own_ref, core_ref, two_ref, two_core_ref, 0, k_win)
    load_window(core, own_ref, core_ref, two_ref, two_core_ref, 1, v_win)
    dk_acc[...] = jnp.zeros_like(dk_acc)
    dv_acc[...] = jnp.zeros_like(dv_acc)
    for tile in range(tiles):
        q_tile = both_heads(q_ref, tile)
        do_tile = both_heads(do_ref, tile)
        at = slice(tile * TILE, (tile + 1) * TILE)
        lse = jnp.concatenate([lse_ref[0:1, at], lse_ref[1:2, at]], axis=1)
        dot = jnp.concatenate([dot_ref[0:1, at], dot_ref[1:2, at]], axis=1)
        for chunk in range(chunks):
            s = band_scores(ctx, tile, chunk, tiles, k_win, q_tile)
            p = jnp.exp2((s - lse) * EXP2_SCALE)
            start = (tile + chunk) * TILE
            dp = mm(v_win[start : start + TILE], do_tile, NT)
            piece = slice(chunk * TILE, (chunk + 1) * TILE)
            p_buf[piece] = p.astype(BF16)
            ds_buf[piece] = (p * (dp - dot)).astype(BF16)
        window = slice(tile * TILE, (tile + chunks) * TILE)
        dv_acc[window] += mm(p_buf[...], do_tile)
        dk_acc[window] += mm(ds_buf[...], q_tile)
        dq = mm(k_win[window], ds_buf[...], TN)
        for r in range(2):
            whole = (dq[:, r * TILE : (r + 1) * TILE] + dq_in_ref[r, :, at]) * SCALE
            dq_ref[at, r * HEAD_SIZE : (r + 1) * HEAD_SIZE] = whole.T.astype(BF16)
    for index, out in ((0, two_out), (1, one_out), (2, own_out)):
        part = slice(index * rows, (index + 1) * rows)
        out[:rows] = (dk_acc[part] * SCALE).astype(BF16)
        out[rows:] = dv_acc[part].astype(BF16)


def load_picked(mine_ref, other_ref, r, part, out):
    size = 4 * BLOCK_TOKENS
    slots = mine_ref.shape[0] // size
    for slot in range(2 * slots):
        source = mine_ref if slot < slots else other_ref
        start = (slot % slots) * size + (2 * r + part) * BLOCK_TOKENS
        out[slot * BLOCK_TOKENS : (slot + 1) * BLOCK_TOKENS] = source[start : start + BLOCK_TOKENS]


def slot_scores(ctx, slot, order, phase, token_start, s):
    owner = slot_owner(ctx, slot, order)
    token = token_start + lax.broadcasted_iota(jnp.int32, s.shape, 1)
    first = jnp.where(owner < ctx - 2, 0, jnp.where(owner == ctx - 2, (STRIDE - 1 - phase) * BLOCK_TOKENS, 2**30))
    return jnp.where(token >= first, s, MASKED)


def stride_forward_kernel(order, phase_ref, q_ref, mine_ref, other_ref, out_in_ref, max_in_ref, sum_in_ref, att_ref, lse_ref, k_pick, v_pick, s_buf, p_buf):
    ctx = lax.axis_index("ctx")
    rows = q_ref.shape[0]
    slots = k_pick.shape[0] // BLOCK_TOKENS
    width = 2 * TILE
    for r in range(2):
        load_picked(mine_ref, other_ref, r, 0, k_pick)
        load_picked(mine_ref, other_ref, r, 1, v_pick)
        for token_start in range(0, rows, width):
            at = slice(token_start, token_start + width)
            q_tile = q_ref[at, r * HEAD_SIZE : (r + 1) * HEAD_SIZE]
            old = max_in_ref[r : r + 1, at]
            top = None
            for slot in range(slots):
                piece = slice(slot * BLOCK_TOKENS, (slot + 1) * BLOCK_TOKENS)
                s = slot_scores(ctx, slot, order, phase_ref[r], token_start, mm(k_pick[piece], q_tile, NT))
                s_buf[piece] = s
                here = jnp.max(s.reshape(BLOCK_TOKENS // 8, 8, width), axis=0)
                top = here if top is None else jnp.maximum(top, here)
            top = jnp.maximum(jnp.max(top, axis=0, keepdims=True), old)
            total = None
            for slot in range(slots):
                piece = slice(slot * BLOCK_TOKENS, (slot + 1) * BLOCK_TOKENS)
                p = jnp.exp2((s_buf[piece] - top) * EXP2_SCALE)
                here = jnp.sum(p.reshape(BLOCK_TOKENS // 8, 8, width), axis=0)
                total = here if total is None else total + here
                p_buf[piece] = p.astype(BF16)
            factor = jnp.exp2((old - top) * EXP2_SCALE)
            total = jnp.sum(total, axis=0, keepdims=True) + sum_in_ref[r : r + 1, at] * factor
            out = mm(v_pick[...], p_buf[...], TN) + out_in_ref[r, :, at] * factor
            out = out / total
            att_ref[at, r * HEAD_SIZE : (r + 1) * HEAD_SIZE] = out.T.astype(BF16)
            lse_ref[r : r + 1, at] = top + jnp.log2(total) * (1.0 / EXP2_SCALE)


def stride_backward_kernel(order, phase_ref, q_ref, grad_own_ref, grad_got_ref, att_ref, lse_ref, mine_ref, other_ref, do_ref, dot_ref, dq_ref, keep_ref, send_ref, k_pick, v_pick, p_buf, ds_buf):
    ctx = lax.axis_index("ctx")
    rows = q_ref.shape[0]
    slots = k_pick.shape[0] // BLOCK_TOKENS
    width = 2 * TILE
    size = 4 * BLOCK_TOKENS
    do_ref[...] = (grad_own_ref[...] + grad_got_ref[...].astype(F32)).astype(BF16)
    for r in range(2):
        head = slice(r * HEAD_SIZE, (r + 1) * HEAD_SIZE)
        product = do_ref[:, head].astype(F32) * att_ref[:, head].astype(F32)
        dot_ref[r : r + 1, :] = jnp.sum(product.T, axis=0, keepdims=True)
        load_picked(mine_ref, other_ref, r, 0, k_pick)
        load_picked(mine_ref, other_ref, r, 1, v_pick)
        for token_start in range(0, rows, width):
            at = slice(token_start, token_start + width)
            q_tile = q_ref[at, head]
            do_tile = do_ref[at, head]
            lse = lse_ref[r : r + 1, at]
            dot = dot_ref[r : r + 1, at]
            for slot in range(slots):
                piece = slice(slot * BLOCK_TOKENS, (slot + 1) * BLOCK_TOKENS)
                s = slot_scores(ctx, slot, order, phase_ref[r], token_start, mm(k_pick[piece], q_tile, NT))
                p = jnp.exp2((s - lse) * EXP2_SCALE)
                dp = mm(v_pick[piece], do_tile, NT)
                p_buf[piece, at] = p.astype(BF16)
                ds_buf[piece, at] = (p * (dp - dot)).astype(BF16)
        dv = mm(p_buf[...], do_ref[:, head])
        dk = mm(ds_buf[...], q_ref[:, head]) * SCALE
        dq_ref[r] = mm(k_pick[...], ds_buf[...], TN)
        for slot in range(slots):
            target = keep_ref if slot < slots // 2 else send_ref
            start = (slot % (slots // 2)) * size + 2 * r * BLOCK_TOKENS
            piece = slice(slot * BLOCK_TOKENS, (slot + 1) * BLOCK_TOKENS)
            target[start : start + BLOCK_TOKENS] = dk[piece].astype(BF16)
            target[start + BLOCK_TOKENS : start + 2 * BLOCK_TOKENS] = dv[piece].astype(BF16)


def finish_kernel(phase_ref, own_ref, core_ref, two_ref, stride_a_ref, stride_b_ref, dk_ref, dv_ref, acc):
    even = lax.axis_index("ctx") % 2 == 0
    rows = dk_ref.shape[0]
    acc[...] = own_ref[...].astype(F32) + two_ref[...].astype(F32) + jnp.where(even, core_ref[...].astype(F32), 0.0)
    stride = stride_a_ref[...].astype(F32) + stride_b_ref[...].astype(F32)
    for r in range(2):
        for part in range(2):
            start = pl.multiple_of(part * rows + (STRIDE - 1 - phase_ref[r]) * BLOCK_TOKENS, BLOCK_TOKENS)
            at = (2 * r + part) * BLOCK_TOKENS
            acc[pl.ds(start, BLOCK_TOKENS)] += stride[at : at + BLOCK_TOKENS]
    dk_ref[...] = acc[:rows].astype(BF16)
    dv_ref[...] = acc[rows:].astype(BF16)


def grad_own_kernel(g_ref, w_ref, out_ref, g_out, w_own, sem):
    width = g_ref.shape[1]
    start = lax.axis_index("head") * width
    step = width // 4
    pairs = []
    for at in range(0, width, step):
        cols = pl.ds(at, step)
        pairs.append((g_ref.at[:, cols], g_out.at[:, cols]))
        pairs.append((w_ref.at[:, pl.ds(pl.multiple_of(start + at, step), step)], w_own.at[:, cols]))
    copies = run_copies(pairs, sem)
    total = None
    for index in range(4):
        copies[2 * index].wait()
        copies[2 * index + 1].wait()
        cols = slice(index * step, (index + 1) * step)
        term = mm(g_out[:, cols], w_own[:, cols], NT)
        total = term if total is None else total + term
    out_ref[...] = total


def grad_other_kernel(g_ref, near_ref, far_ref, out_ref):
    core = lax.axis_index("ctx") % 2
    width = near_ref.shape[1]
    near = pl.ds(pl.multiple_of(core * width, width), width)
    far = pl.ds(pl.multiple_of((1 - core) * width, width), width)
    total = mm(g_ref[:, near], near_ref[...], NT) + mm(g_ref[:, far], far_ref[...], NT)
    out_ref[...] = total.astype(BF16)


def layer_out_kernel(own_ref, other_ref, w_ref, near_ref, far_ref, out_ref):
    core = lax.axis_index("ctx") % 2
    width = near_ref.shape[1]
    step = min(width, 256)
    for part, source in ((core, near_ref), (1 - core, far_ref)):
        for at in range(0, width, step):
            cols = pl.ds(pl.multiple_of(part * width + at, step), step)
            total = mm(own_ref[...], w_ref[:, cols]) + mm(other_ref[...], source[:, at : at + step])
            out_ref[:, cols] = total.astype(BF16)


def weight_grad_kernel(bits, att_ref, g_ref, keep_ref, send_ref):
    ctx = lax.axis_index("ctx")
    _, _, cols = keep_ref.shape
    blocks = 1 << len(bits)
    att = att_ref[...].T
    for slot in range(blocks):
        mask = 0
        for k, bit in enumerate(bits):
            if slot >> (len(bits) - 1 - k) & 1:
                mask |= bit
        block = (ctx % blocks) ^ mask
        term = mm(att, g_ref[:, pl.ds(pl.multiple_of(block * cols, cols), cols)]).astype(BF16)
        if slot < blocks // 2:
            keep_ref[slot] = term
        else:
            send_ref[slot - blocks // 2] = term


def halve_kernel(keep_ref, got_ref, keep_out, send_out):
    middle = keep_out.shape[0]
    keep_out[...] = keep_ref[:middle].astype(F32) + got_ref[:middle].astype(F32)
    send_out[...] = (keep_ref[middle:].astype(F32) + got_ref[middle:].astype(F32)).astype(BF16)


def halve(run, name, keep, got, after=()):
    half = (keep.shape[0] // 2,) + keep.shape[1:]
    return run(halve_kernel, name, [keep, got], [shape(half, F32), shape(half, BF16)], after=after)


def add_kernel(core, left_ref, right_ref, out_ref):
    here = lax.axis_index("ctx") % 2 == core
    left = left_ref[...].astype(F32)
    out_ref[...] = jnp.where(here, left + right_ref[...].astype(F32), left).astype(BF16)


def end_kernel(left_ref, right_ref, low_ref):
    low_ref[...] = (left_ref[0].astype(F32) + right_ref[0].astype(F32)).astype(BF16)


def choose_kernel(own_ref, own_got_ref, other_ref, keep_ref, send_ref):
    same = lax.axis_index("ctx") // (lax.axis_size("ctx") // 2) == lax.axis_index("head")
    own = own_ref[0].astype(F32) + own_got_ref[0].astype(F32)
    other = other_ref[...].astype(F32)
    keep_ref[...] = jnp.where(same, own, other)
    send_ref[...] = jnp.where(same, other, own).astype(BF16)


def last_sum_kernel(keep_ref, got_ref, out_ref):
    out_ref[...] = (keep_ref[...] + got_ref[...].astype(F32)).astype(BF16)


def body(queries, rotated_key_rows, value_head_rows, stride_offset, w_out, grad_out):
    rows = queries.shape[0]
    n_ctx = lax.axis_size("ctx")
    n_head = lax.axis_size("head")
    model = w_out.shape[1]
    width = grad_out.shape[1]
    head_rows = w_out.shape[0]
    ratio = n_ctx // n_head
    cols = model // n_ctx
    pair = n_head == 2
    flip = functools.partial(flips, n_ctx)
    swap = [(0, 1), (1, 0)]
    scores = rows * 2 * HEAD_SIZE * 2
    proj = 2 * rows * head_rows * width
    run = Sequence()

    packed = run(
        pack_kernel, "pack",
        [stride_offset, rotated_key_rows, value_head_rows] + ([w_out] if pair else []),
        [shape((2 * rows, HEAD_SIZE), BF16), shape((4 * BLOCK_TOKENS, HEAD_SIZE), BF16)]
        + ([shape((head_rows, width // 2), BF16)] if pair else []),
        [pltpu.VMEM((2 * rows, HEAD_SIZE), BF16)]
        + ([pltpu.VMEM((head_rows, width // 2), BF16)] if pair else [])
        + [pltpu.SemaphoreType.DMA((3,)), pltpu.SemaphoreType.DMA((6,))],
        far=(1, 2, 3) if pair else (1, 2), mib=60, out_space=HBM,
    )
    run.last = []
    kv, picks = packed[:2]
    if pair:
        w_near = lax.ppermute(packed[2], "head", swap)
    else:
        w_all = lax.all_to_all(w_out, "head", 1, 0, tiled=True)
    order = []
    bit = 4
    while bit < n_ctx:
        order.append(bit)
        bit *= 2
    order = tuple(order + [2, 1])
    picks_got = lax.ppermute(picks, "ctx", flip(order[0]))
    kv_two = lax.ppermute(kv, "ctx", [(i, i + 2) for i in range(n_ctx - 2)])
    kv_core = lax.ppermute(kv, "ctx", flip(1))
    picks = join(run, "stride_join", picks, picks_got)
    picks_got = lax.ppermute(picks, "ctx", flip(order[1]))
    if pair:
        grad_own, grad_out, w_own = run(
            grad_own_kernel, "grad_own", [grad_out, w_out],
            [shape((rows, head_rows), F32), shape(grad_out.shape, BF16), shape((head_rows, width), BF16)],
            [pltpu.SemaphoreType.DMA((8,))], flops=proj, after=[kv_core], far=(0, 1),
        )
    for bit in order[2:-1]:
        picks = join(run, "stride_join", picks, picks_got)
        picks_got = lax.ppermute(picks, "ctx", flip(bit))
    kv_two = run.hold(kv_two)
    kv_two_core = lax.ppermute(kv_two, "ctx", flip(1))

    chunk_rows = (2 * (rows // TILE) + 1) * TILE
    window = pltpu.VMEM((3 * rows, HEAD_SIZE), BF16)
    picked_rows = n_ctx * BLOCK_TOKENS
    pick = pltpu.VMEM((picked_rows, HEAD_SIZE), BF16)
    out, top, total = run(
        band_forward_kernel, "band_forward", [queries, kv, kv_core, kv_two, kv_two_core],
        [shape((2, HEAD_SIZE, rows), F32), shape((2, rows), F32), shape((2, rows), F32)],
        [window, window, pltpu.VMEM((chunk_rows, 2 * TILE), F32), pltpu.VMEM((chunk_rows, 2 * TILE), BF16)],
        flops=2 * scores * chunk_rows,
    )
    picks = join(run, "stride_join", picks, picks_got)
    picks_other = lax.ppermute(picks, "ctx", flip(1))
    if pair:
        w_near = run.hold(w_near)
        w_far = lax.ppermute(w_near, "ctx", flip(1))
        grad_other, = run(
            grad_other_kernel, "grad_other", [grad_out, w_near, w_far],
            [shape((rows, head_rows), BF16)], flops=proj,
        )
        grad_got = lax.ppermute(grad_other, "head", swap)
    if not pair:
        grad_all = mm(grad_out, w_all, NT).astype(BF16)
        grad_all = lax.all_to_all(grad_all.reshape(rows, n_head, head_rows), "head", 1, 0, tiled=True)
        grad_all = grad_all.reshape(n_head, rows, head_rows).astype(F32)
        grad_own = jnp.sum(grad_all, axis=0)
        grad_got = jnp.zeros((rows, head_rows), BF16)
    attended, lse = run(
        functools.partial(stride_forward_kernel, order), "stride_forward",
        [stride_offset, queries, picks, picks_other, out, top, total],
        [shape((rows, head_rows), BF16), shape((2, rows), F32)],
        [pick, pick, pltpu.VMEM((picked_rows, 2 * TILE), F32), pltpu.VMEM((picked_rows, 2 * TILE), BF16)],
        flops=2 * scores * picked_rows,
    )
    if pair:
        att_other = lax.ppermute(attended, "head", swap)
        bits = [1]
        while 2 * bits[-1] < ratio:
            bits.append(2 * bits[-1])
        own_bits = tuple(bits[:1] + bits[:0:-1])
        other_bits = tuple(bits)

        def weight_grad(source, name, bits):
            part = shape((ratio // 2, head_rows, cols), BF16)
            return run(
                functools.partial(weight_grad_kernel, bits), name, [source, grad_out], [part, part], flops=proj
            )

        own_keep, own_send = weight_grad(attended, "weight_grad_own", own_bits)
        own_got = lax.ppermute(own_send, "ctx", flip(1))
    grad_att, row_dot, grad_q, stride_keep, stride_send = run(
        functools.partial(stride_backward_kernel, order), "stride_backward",
        [stride_offset, queries, grad_own, grad_got, attended, lse, picks, picks_other],
        [
            shape((rows, head_rows), BF16), shape((2, rows), F32), shape((2, HEAD_SIZE, rows), F32),
            shape(picks.shape, BF16), shape(picks.shape, BF16),
        ],
        [pick, pick, pltpu.VMEM((picked_rows, rows), BF16), pltpu.VMEM((picked_rows, rows), BF16)],
        flops=5 * scores * picked_rows,
    )
    stride_got = lax.ppermute(stride_send, "ctx", flip(1))
    if pair:
        own_keep, own_send = halve(run, "weight_grad_own_core", own_keep, own_got, after=[att_other])
        own_got = lax.ppermute(own_send, "ctx", flip(own_bits[1]))
        other_keep, other_send = weight_grad(att_other, "weight_grad_other", other_bits)
        other_got = lax.ppermute(other_send, "ctx", flip(1))
    stride_keep, stride_send = halve(run, "stride_core", stride_keep, stride_got)
    stride_got = lax.ppermute(stride_send, "ctx", flip(2))
    if pair:
        other_keep, other_send = halve(run, "weight_grad_other_core", other_keep, other_got)
        other_got = lax.ppermute(other_send, "ctx", flip(other_bits[1]))
    grad_queries, own, one, two = run(
        band_backward_kernel, "band_backward",
        [queries, grad_att, kv, kv_core, kv_two, kv_two_core, lse, row_dot, grad_q],
        [shape((rows, head_rows), BF16)] + [shape((2 * rows, HEAD_SIZE), BF16)] * 3,
        [
            window, window, pltpu.VMEM((3 * rows, HEAD_SIZE), F32), pltpu.VMEM((3 * rows, HEAD_SIZE), F32),
            pltpu.VMEM((chunk_rows, 2 * TILE), BF16), pltpu.VMEM((chunk_rows, 2 * TILE), BF16),
        ],
        flops=5 * scores * chunk_rows,
    )
    one_got = lax.ppermute(one, "ctx", flip(1))
    stride_bits = list(reversed(order))[1:]
    if pair:
        for bit in own_bits[2:]:
            own_keep, own_send = halve(run, "weight_grad_own_low", own_keep, own_got)
            own_got = lax.ppermute(own_send, "ctx", flip(bit))
    stride_keep, stride_send = halve(run, "stride_y", stride_keep, stride_got)
    stride_got = lax.ppermute(stride_send, "ctx", flip(stride_bits[1]))
    if pair:
        for bit in other_bits[2:]:
            other_keep, other_send = halve(run, "weight_grad_other_low", other_keep, other_got)
            other_got = lax.ppermute(other_send, "ctx", flip(bit))
    two, = run(functools.partial(add_kernel, 1), "band_two", [two, one_got], [shape(two.shape, BF16)])
    two_got = lax.ppermute(two, "ctx", [(i + 2, i) for i in range(n_ctx - 2)])
    if pair:
        layer_out, = run(
            layer_out_kernel, "layer_out", [attended, att_other, w_own, w_near, w_far],
            [shape((rows, width), BF16)], flops=2 * proj,
        )
    for bit in stride_bits[2:]:
        stride_keep, stride_send = halve(run, "stride_z", stride_keep, stride_got)
        stride_got = lax.ppermute(stride_send, "ctx", flip(bit))
    if pair:
        block = (head_rows, cols)
        other_low, = run(end_kernel, "weight_grad_other_end", [other_keep, other_got], [shape(block, BF16)])
        other_got = lax.ppermute(other_low, "head", swap)
        sum_keep, sum_send = run(
            choose_kernel, "choose", [own_keep, own_got, other_got], [shape(block, F32), shape(block, BF16)]
        )
        sum_got = lax.ppermute(sum_send, "ctx", flip(n_ctx // 2))
    else:
        att_all = lax.all_gather(attended, "head", axis=1, tiled=True)
        layer_out = mm(att_all, w_all).astype(BF16)
        terms = mm(att_all, grad_out, TN).astype(BF16).reshape(n_head, head_rows, ratio, cols)
        terms = jnp.transpose(terms, (0, 2, 1, 3)).reshape(n_ctx, head_rows, cols)
        terms = lax.psum_scatter(terms, "ctx", scatter_dimension=0, tiled=True)[0]
        route = []
        for c in range(n_ctx):
            for h in range(n_head):
                target = (h * ratio + c % ratio) * n_head + c // ratio
                route.append((c * n_head + h, target))
        grad_w_out = lax.ppermute(terms, ("ctx", "head"), route)

    key_gradient, value_gradient = run(
        finish_kernel, "finish", [stride_offset, own, one_got, two_got, stride_keep, stride_got],
        [shape((rows, HEAD_SIZE), BF16)] * 2,
        [pltpu.VMEM((2 * rows, HEAD_SIZE), F32)],
    )
    if pair:
        grad_w_out, = run(last_sum_kernel, "last_sum", [sum_keep, sum_got], [shape(block, BF16)])
    return (layer_out, grad_queries, key_gradient, value_gradient, grad_w_out)


def solution(mesh):
    placed = (
        P("ctx", "head"),
        P("ctx", "head"),
        P("ctx", "head"),
        P("head"),
        P("head", None),
        P("ctx", "head"),
    )
    return jax.shard_map(
        body,
        mesh=mesh,
        in_specs=placed,
        out_specs=(
            P("ctx", "head"),
            P("ctx", "head"),
            P("ctx", "head"),
            P("ctx", "head"),
            P("head", "ctx"),
        ),
        check_vma=False,
    )
```

```python
import functools
import math

import jax
import jax.numpy as jnp
from jax import lax
from jax.experimental import pallas as pl
from jax.experimental.pallas import tpu as pltpu
from jax.sharding import PartitionSpec as P

HEAD_SIZE = 128
BLOCK_TOKENS = 64
LOCAL = 16
STRIDE = 8
TILE = 128
BF16 = jnp.bfloat16
F32 = jnp.float32
SCALE = HEAD_SIZE ** (-0.5)
EXP2_SCALE = SCALE * math.log2(math.e)
MASKED = -1e30

VMEM = pl.BlockSpec(memory_space=pltpu.VMEM)
ANY = pl.BlockSpec(memory_space=pl.ANY)
HBM = pl.BlockSpec(memory_space=pltpu.HBM)
SMEM = pl.BlockSpec(memory_space=pltpu.SMEM)
NN = (((1,), (0,)), ((), ()))
NT = (((1,), (1,)), ((), ()))
TN = (((0,), (0,)), ((), ()))


def mm(left, right, dims=NN):
    return lax.dot_general(left, right, dims, preferred_element_type=F32)


USEC = {'pack': 2, 'grad_own': 2, 'grad_other': 0.1, 'band_forward': 2.7, 'stride_forward': 36, 'stride_backward': 46, 'band_backward': 40, 'layer_out': 26, 'finish': 0.1, 'last_sum': 7, 'weight_grad_own': 8, 'weight_grad_other': 8, 'hold_grad': 10, 'weight_grad_own_low': 10}


class Sequence:
    def __init__(self):
        self.last = []

    def __call__(self, kernel, name, ins, out_shapes, scratch=(), mib=32, flops=0, after=(), far=(), out_space=VMEM):
        extra = self.last + list(after)
        count = len(ins)

        def wrapped(*refs):
            rest = refs[count + len(extra) :]
            kernel(*refs[:count], *rest[: len(out_shapes)], *rest[len(out_shapes) + 1 :])
            token = rest[len(out_shapes)]
            token[...] = jnp.zeros_like(token)

        specs = [SMEM if a.ndim == 1 else VMEM for a in ins]
        for index in far:
            specs[index] = HBM
        outs = pl.pallas_call(
            wrapped,
            name=name,
            out_shape=list(out_shapes) + [shape((8, 128), F32)],
            in_specs=specs + [ANY] * len(extra),
            out_specs=[out_space] * len(out_shapes) + [VMEM],
            scratch_shapes=list(scratch),
            compiler_params=pltpu.CompilerParams(vmem_limit_bytes=mib * 2**20),
            cost_estimate=pl.CostEstimate(flops=int(1e9 * USEC.get(name, 0.1)), bytes_accessed=1, transcendentals=0),
        )(*ins, *extra)
        self.last = [outs[-1]]
        return outs[:-1]


    def hold(self, array, name="hold"):
        extra = self.last

        def kernel(*refs):
            token = refs[-1]
            token[...] = jnp.zeros_like(token)

        held, token = pl.pallas_call(
            kernel,
            name=name,
            out_shape=[shape(array.shape, array.dtype), shape((8, 128), F32)],
            in_specs=[ANY] * (1 + len(extra)),
            out_specs=[ANY, VMEM],
            input_output_aliases={0: 0},
            compiler_params=pltpu.CompilerParams(vmem_limit_bytes=2**20),
            cost_estimate=pl.CostEstimate(flops=int(1e9 * USEC.get(name, 0.1)), bytes_accessed=1, transcendentals=0),
        )(array, *extra)
        self.last = [token]
        return held


def shape(dims, dtype):
    return jax.ShapeDtypeStruct(dims, dtype)


def flips(count, bit):
    return [(i, i ^ bit) for i in range(count)]


def slot_owner(ctx, slot, order):
    mask = 0
    for k, bit in enumerate(order):
        if slot >> k & 1:
            mask |= bit
    return ctx ^ mask


def run_copies(pairs, sem):
    copies = [pltpu.make_async_copy(src, dst, sem.at[i]) for i, (src, dst) in enumerate(pairs)]
    for copy in copies:
        copy.start()
    return copies


def pack_kernel(phase_ref, k_ref, v_ref, *refs):
    if len(refs) == 4:
        kv_ref, pick_ref, phases, sem = refs
        pairs = []
    else:
        w_ref, kv_ref, pick_ref, piece_ref, phases, sem = refs
        cols = piece_ref.shape[1]
        start = (1 - lax.axis_index("head")) * 2 * cols + lax.axis_index("ctx") % 2 * cols
        pairs = [(w_ref.at[:, pl.ds(pl.multiple_of(start, cols), cols)], piece_ref)]
    rows = k_ref.shape[0]
    pairs = [(phase_ref, phases), (k_ref, kv_ref.at[pl.ds(0, rows)]), (v_ref, kv_ref.at[pl.ds(rows, rows)])] + pairs
    copies = run_copies(pairs, sem)
    for copy in copies[:3]:
        copy.wait()
    for r in range(2):
        for part in range(2):
            start = pl.multiple_of(part * rows + (STRIDE - 1 - phases[r]) * BLOCK_TOKENS, BLOCK_TOKENS)
            at = (2 * r + part) * BLOCK_TOKENS
            pick_ref[at : at + BLOCK_TOKENS] = kv_ref[pl.ds(start, BLOCK_TOKENS)]
    for copy in copies[3:]:
        copy.wait()


def join_kernel(first_ref, second_ref, out_ref):
    middle = first_ref.shape[0]
    out_ref[:middle] = first_ref[...]
    out_ref[middle:] = second_ref[...]


def join(run, name, first, second, after=()):
    return run(join_kernel, name, [first, second], [shape((2 * first.shape[0],) + first.shape[1:], BF16)], after=after)[0]


def load_window(core, own_ref, core_ref, two_ref, two_core_ref, part, out):
    rows = own_ref.shape[0] // 2
    piece = pl.ds(part * rows, rows)
    out[:rows] = two_ref[piece]
    out[rows : 2 * rows] = jnp.where(core == 0, two_core_ref[piece], core_ref[piece])
    out[2 * rows :] = own_ref[piece]


def band_scores(ctx, tile, chunk, tiles, k_win, q_tile):
    start = (tile + chunk) * TILE
    s = mm(k_win[start : start + TILE], q_tile, NT)
    if chunk == 0 or chunk == 2 * tiles:
        key = lax.broadcasted_iota(jnp.int32, s.shape, 0)
        token = lax.broadcasted_iota(jnp.int32, s.shape, 1) % TILE
        if chunk == 0:
            s = jnp.where(key // BLOCK_TOKENS > token // BLOCK_TOKENS, s, MASKED)
        else:
            s = jnp.where(key <= token, s, MASKED)
    if tile + chunk < 2 * tiles:
        first = 2 - (tile + chunk) // tiles
        s = jnp.where(ctx >= first, s, MASKED)
    return s


def both_heads(ref, tile):
    rows = slice(tile * TILE, (tile + 1) * TILE)
    return jnp.concatenate([ref[rows, :HEAD_SIZE], ref[rows, HEAD_SIZE:]], axis=0)


def band_forward_kernel(phase_ref, q_ref, own_ref, core_ref, two_ref, two_core_ref, out_ref, max_ref, sum_ref, first_ref, k_win, v_win, s_buf, p_buf):
    ctx = lax.axis_index("ctx")
    core = ctx % 2
    tiles = q_ref.shape[0] // TILE
    chunks = 2 * tiles + 1
    load_window(core, own_ref, core_ref, two_ref, two_core_ref, 0, k_win)
    load_window(core, own_ref, core_ref, two_ref, two_core_ref, 1, v_win)
    for r in range(2):
        first_ref[r : r + 1, :] = jnp.full((1, first_ref.shape[1]), (STRIDE - 1 - phase_ref[r]) * BLOCK_TOKENS, jnp.int32)
    for tile in range(tiles):
        q_tile = both_heads(q_ref, tile)
        top = None
        for chunk in range(chunks):
            s = band_scores(ctx, tile, chunk, tiles, k_win, q_tile)
            s_buf[chunk * TILE : (chunk + 1) * TILE] = s
            here = jnp.max(s.reshape(TILE // 8, 8, 2 * TILE), axis=0)
            top = here if top is None else jnp.maximum(top, here)
        top = jnp.max(top, axis=0, keepdims=True)
        total = None
        for chunk in range(chunks):
            p = jnp.exp2((s_buf[chunk * TILE : (chunk + 1) * TILE] - top) * EXP2_SCALE)
            here = jnp.sum(p.reshape(TILE // 8, 8, 2 * TILE), axis=0)
            total = here if total is None else total + here
            p_buf[chunk * TILE : (chunk + 1) * TILE] = p.astype(BF16)
        total = jnp.sum(total, axis=0, keepdims=True)
        out = mm(v_win[tile * TILE : (tile + chunks) * TILE], p_buf[...], TN)
        at = slice(tile * TILE, (tile + 1) * TILE)
        for r in range(2):
            half = slice(r * TILE, (r + 1) * TILE)
            out_ref[r, :, at] = out[:, half]
            max_ref[r : r + 1, at] = top[:, half]
            sum_ref[r : r + 1, at] = total[:, half]


def band_backward_kernel(
    q_ref, do_ref, own_ref, core_ref, two_ref, two_core_ref, lse_ref, dot_ref, dq_in_ref,
    dq_ref, own_out, one_out, two_out, k_win, v_win, dk_acc, dv_acc, p_buf, ds_buf,
):
    ctx = lax.axis_index("ctx")
    core = ctx % 2
    rows = q_ref.shape[0]
    tiles = rows // TILE
    chunks = 2 * tiles + 1
    load_window(core, own_ref, core_ref, two_ref, two_core_ref, 0, k_win)
    load_window(core, own_ref, core_ref, two_ref, two_core_ref, 1, v_win)
    dk_acc[...] = jnp.zeros_like(dk_acc)
    dv_acc[...] = jnp.zeros_like(dv_acc)
    for tile in range(tiles):
        q_tile = both_heads(q_ref, tile)
        do_tile = both_heads(do_ref, tile)
        at = slice(tile * TILE, (tile + 1) * TILE)
        lse = jnp.concatenate([lse_ref[0:1, at], lse_ref[1:2, at]], axis=1)
        dot = jnp.concatenate([dot_ref[0:1, at], dot_ref[1:2, at]], axis=1)
        for chunk in range(chunks):
            s = band_scores(ctx, tile, chunk, tiles, k_win, q_tile)
            p = jnp.exp2((s - lse) * EXP2_SCALE)
            start = (tile + chunk) * TILE
            dp = mm(v_win[start : start + TILE], do_tile, NT)
            piece = slice(chunk * TILE, (chunk + 1) * TILE)
            p_buf[piece] = p.astype(BF16)
            ds_buf[piece] = (p * (dp - dot)).astype(BF16)
        window = slice(tile * TILE, (tile + chunks) * TILE)
        dv_acc[window] += mm(p_buf[...], do_tile)
        dk_acc[window] += mm(ds_buf[...], q_tile)
        dq = mm(k_win[window], ds_buf[...], TN)
        for r in range(2):
            whole = (dq[:, r * TILE : (r + 1) * TILE] + dq_in_ref[r, :, at]) * SCALE
            dq_ref[at, r * HEAD_SIZE : (r + 1) * HEAD_SIZE] = whole.T.astype(BF16)
    for index, out in ((0, two_out), (1, one_out), (2, own_out)):
        part = slice(index * rows, (index + 1) * rows)
        out[:rows] = (dk_acc[part] * SCALE).astype(BF16)
        out[rows:] = dv_acc[part].astype(BF16)


def load_picked(mine_ref, other_ref, r, part, out):
    size = 4 * BLOCK_TOKENS
    slots = mine_ref.shape[0] // size
    for slot in range(2 * slots):
        source = mine_ref if slot < slots else other_ref
        start = (slot % slots) * size + (2 * r + part) * BLOCK_TOKENS
        out[slot * BLOCK_TOKENS : (slot + 1) * BLOCK_TOKENS] = source[start : start + BLOCK_TOKENS]


def slot_scores(ctx, slot, order, nearest, token_start, s):
    owner = slot_owner(ctx, slot, order)
    token = token_start + lax.broadcasted_iota(jnp.int32, s.shape, 1)
    first = jnp.where(owner < ctx - 2, 0, jnp.where(owner == ctx - 2, nearest, 2**30))
    return jnp.where(token >= first, s, MASKED)


def stride_forward_kernel(order, first_ref, q_ref, mine_ref, other_ref, out_in_ref, max_in_ref, sum_in_ref, att_ref, lse_ref, k_pick, v_pick, s_buf, p_buf):
    ctx = lax.axis_index("ctx")
    rows = q_ref.shape[0]
    slots = k_pick.shape[1] // BLOCK_TOKENS
    width = 2 * TILE
    steps = [(r, token_start) for r in range(2) for token_start in range(0, rows, width)]
    for r in range(2):
        load_picked(mine_ref, other_ref, r, 0, k_pick.at[r])
        load_picked(mine_ref, other_ref, r, 1, v_pick.at[r])

    def scores(step):
        r, token_start = steps[step]
        q_tile = q_ref[token_start : token_start + width, r * HEAD_SIZE : (r + 1) * HEAD_SIZE]
        s_buf[step] = mm(k_pick[r], q_tile, NT)

    def weigh(step):
        r, token_start = steps[step]
        at = slice(token_start, token_start + width)
        old = max_in_ref[r : r + 1, at]
        top = None
        for slot in range(slots):
            piece = slice(slot * BLOCK_TOKENS, (slot + 1) * BLOCK_TOKENS)
            s = slot_scores(ctx, slot, order, first_ref[r : r + 1, at], token_start, s_buf[step, piece])
            s_buf[step, piece] = s
            here = jnp.max(s.reshape(BLOCK_TOKENS // 8, 8, width), axis=0)
            top = here if top is None else jnp.maximum(top, here)
        top = jnp.maximum(jnp.max(top, axis=0, keepdims=True), old)
        total = None
        for slot in range(slots):
            piece = slice(slot * BLOCK_TOKENS, (slot + 1) * BLOCK_TOKENS)
            p = jnp.exp2((s_buf[step, piece] - top) * EXP2_SCALE)
            here = jnp.sum(p.reshape(BLOCK_TOKENS // 8, 8, width), axis=0)
            total = here if total is None else total + here
            p_buf[step, piece] = p.astype(BF16)
        factor = jnp.exp2((old - top) * EXP2_SCALE)
        total = jnp.sum(total, axis=0, keepdims=True) + sum_in_ref[r : r + 1, at] * factor
        lse_ref[r : r + 1, at] = top + jnp.log2(total) * (1.0 / EXP2_SCALE)
        return factor, total

    def mix(step, factor, total):
        r, token_start = steps[step]
        at = slice(token_start, token_start + width)
        out = mm(v_pick[r], p_buf[step], TN) + out_in_ref[r, :, at] * factor
        att_ref[at, r * HEAD_SIZE : (r + 1) * HEAD_SIZE] = (out / total).T.astype(BF16)

    scores(0)
    for step in range(len(steps)):
        if step + 1 < len(steps):
            scores(step + 1)
        mix(step, *weigh(step))


def stride_backward_kernel(order, first_ref, q_ref, grad_own_ref, grad_got_ref, att_ref, lse_ref, mine_ref, other_ref, do_ref, dot_ref, dq_ref, keep_ref, send_ref, k_pick, v_pick, p_buf, ds_buf, s_buf, dp_buf):
    ctx = lax.axis_index("ctx")
    rows = q_ref.shape[0]
    slots = k_pick.shape[0] // BLOCK_TOKENS
    width = 2 * TILE
    size = 4 * BLOCK_TOKENS
    do_ref[...] = (grad_own_ref[...] + grad_got_ref[...].astype(F32)).astype(BF16)
    for r in range(2):
        head = slice(r * HEAD_SIZE, (r + 1) * HEAD_SIZE)
        product = do_ref[:, head].astype(F32) * att_ref[:, head].astype(F32)
        dot_ref[r : r + 1, :] = jnp.sum(product.T, axis=0, keepdims=True)
        load_picked(mine_ref, other_ref, r, 0, k_pick)
        load_picked(mine_ref, other_ref, r, 1, v_pick)
        for token_start in range(0, rows, width):
            at = slice(token_start, token_start + width)
            q_tile = q_ref[at, head]
            do_tile = do_ref[at, head]
            lse = lse_ref[r : r + 1, at]
            dot = dot_ref[r : r + 1, at]
            s_buf[...] = mm(k_pick[...], q_tile, NT)
            dp_buf[...] = mm(v_pick[...], do_tile, NT)
            for slot in range(slots):
                piece = slice(slot * BLOCK_TOKENS, (slot + 1) * BLOCK_TOKENS)
                s = slot_scores(ctx, slot, order, first_ref[r : r + 1, at], token_start, s_buf[piece])
                p = jnp.exp2((s - lse) * EXP2_SCALE)
                p_buf[piece, at] = p.astype(BF16)
                ds_buf[piece, at] = (p * (dp_buf[piece] - dot)).astype(BF16)
        dv = mm(p_buf[...], do_ref[:, head])
        dk = mm(ds_buf[...], q_ref[:, head]) * SCALE
        dq_ref[r] = mm(k_pick[...], ds_buf[...], TN)
        for slot in range(slots):
            target = keep_ref if slot < slots // 2 else send_ref
            start = (slot % (slots // 2)) * size + 2 * r * BLOCK_TOKENS
            piece = slice(slot * BLOCK_TOKENS, (slot + 1) * BLOCK_TOKENS)
            target[start : start + BLOCK_TOKENS] = dk[piece].astype(BF16)
            target[start + BLOCK_TOKENS : start + 2 * BLOCK_TOKENS] = dv[piece].astype(BF16)


def finish_kernel(phase_ref, own_ref, core_ref, two_ref, stride_a_ref, stride_b_ref, dk_ref, dv_ref, acc):
    even = lax.axis_index("ctx") % 2 == 0
    rows = dk_ref.shape[0]
    acc[...] = own_ref[...].astype(F32) + two_ref[...].astype(F32) + jnp.where(even, core_ref[...].astype(F32), 0.0)
    stride = stride_a_ref[...].astype(F32) + stride_b_ref[...].astype(F32)
    for r in range(2):
        for part in range(2):
            start = pl.multiple_of(part * rows + (STRIDE - 1 - phase_ref[r]) * BLOCK_TOKENS, BLOCK_TOKENS)
            at = (2 * r + part) * BLOCK_TOKENS
            acc[pl.ds(start, BLOCK_TOKENS)] += stride[at : at + BLOCK_TOKENS]
    dk_ref[...] = acc[:rows].astype(BF16)
    dv_ref[...] = acc[rows:].astype(BF16)


def grad_own_kernel(g_ref, w_ref, out_ref, g_out, w_own, sem):
    width = g_ref.shape[1]
    start = lax.axis_index("head") * width
    step = width // 4
    pairs = []
    for at in range(0, width, step):
        cols = pl.ds(at, step)
        pairs.append((g_ref.at[:, cols], g_out.at[:, cols]))
        pairs.append((w_ref.at[:, pl.ds(pl.multiple_of(start + at, step), step)], w_own.at[:, cols]))
    copies = run_copies(pairs, sem)
    total = None
    for index in range(4):
        copies[2 * index].wait()
        copies[2 * index + 1].wait()
        cols = slice(index * step, (index + 1) * step)
        term = mm(g_out[:, cols], w_own[:, cols], NT)
        total = term if total is None else total + term
    out_ref[...] = total


def grad_other_kernel(g_ref, near_ref, far_ref, out_ref):
    core = lax.axis_index("ctx") % 2
    width = near_ref.shape[1]
    near = pl.ds(pl.multiple_of(core * width, width), width)
    far = pl.ds(pl.multiple_of((1 - core) * width, width), width)
    total = mm(g_ref[:, near], near_ref[...], NT) + mm(g_ref[:, far], far_ref[...], NT)
    out_ref[...] = total.astype(BF16)


def layer_out_kernel(own_ref, other_ref, w_ref, near_ref, far_ref, out_ref):
    core = lax.axis_index("ctx") % 2
    width = near_ref.shape[1]
    step = min(width, 256)
    for part, source in ((core, near_ref), (1 - core, far_ref)):
        for at in range(0, width, step):
            cols = pl.ds(pl.multiple_of(part * width + at, step), step)
            total = mm(own_ref[...], w_ref[:, cols]) + mm(other_ref[...], source[:, at : at + step])
            out_ref[:, cols] = total.astype(BF16)


def weight_grad_kernel(bits, att_ref, g_ref, keep_ref, send_ref):
    ctx = lax.axis_index("ctx")
    _, _, cols = keep_ref.shape
    blocks = 1 << len(bits)
    att = att_ref[...].T
    for slot in range(blocks):
        mask = 0
        for k, bit in enumerate(bits):
            if slot >> (len(bits) - 1 - k) & 1:
                mask |= bit
        block = (ctx % blocks) ^ mask
        term = mm(att, g_ref[:, pl.ds(pl.multiple_of(block * cols, cols), cols)]).astype(BF16)
        if slot < blocks // 2:
            keep_ref[slot] = term
        else:
            send_ref[slot - blocks // 2] = term


def halve_kernel(keep_ref, got_ref, keep_out, send_out):
    middle = keep_out.shape[0]
    keep_out[...] = keep_ref[:middle].astype(F32) + got_ref[:middle].astype(F32)
    send_out[...] = (keep_ref[middle:].astype(F32) + got_ref[middle:].astype(F32)).astype(BF16)


def halve(run, name, keep, got, after=()):
    half = (keep.shape[0] // 2,) + keep.shape[1:]
    return run(halve_kernel, name, [keep, got], [shape(half, F32), shape(half, BF16)], after=after)


def add_kernel(core, left_ref, right_ref, out_ref):
    here = lax.axis_index("ctx") % 2 == core
    left = left_ref[...].astype(F32)
    out_ref[...] = jnp.where(here, left + right_ref[...].astype(F32), left).astype(BF16)


def end_kernel(left_ref, right_ref, low_ref):
    low_ref[...] = (left_ref[0].astype(F32) + right_ref[0].astype(F32)).astype(BF16)


def choose_kernel(own_ref, other_ref, keep_ref, send_ref):
    same = lax.axis_index("ctx") // (lax.axis_size("ctx") // 2) == lax.axis_index("head")
    keep_ref[...] = jnp.where(same, own_ref[...], other_ref[...])
    send_ref[...] = jnp.where(same, other_ref[...], own_ref[...])


def last_sum_kernel(keep_ref, got_ref, out_ref):
    out_ref[...] = (keep_ref[...].astype(F32) + got_ref[...].astype(F32)).astype(BF16)


def body(queries, rotated_key_rows, value_head_rows, stride_offset, w_out, grad_out):
    rows = queries.shape[0]
    n_ctx = lax.axis_size("ctx")
    n_head = lax.axis_size("head")
    model = w_out.shape[1]
    width = grad_out.shape[1]
    head_rows = w_out.shape[0]
    ratio = n_ctx // n_head
    cols = model // n_ctx
    pair = n_head == 2
    flip = functools.partial(flips, n_ctx)
    swap = [(0, 1), (1, 0)]
    scores = rows * 2 * HEAD_SIZE * 2
    proj = 2 * rows * head_rows * width
    run = Sequence()

    packed = run(
        pack_kernel, "pack",
        [stride_offset, rotated_key_rows, value_head_rows] + ([w_out] if pair else []),
        [shape((2 * rows, HEAD_SIZE), BF16), shape((4 * BLOCK_TOKENS, HEAD_SIZE), BF16)]
        + ([shape((head_rows, width // 2), BF16)] if pair else []),
        [pltpu.SMEM((2,), jnp.int32), pltpu.SemaphoreType.DMA((4,))], far=(0, 1, 2, 3) if pair else (0, 1, 2), mib=54,
    )
    run.last = []
    kv, picks = packed[:2]
    if pair:
        w_near = lax.ppermute(packed[2], "head", swap)
    else:
        w_all = lax.all_to_all(w_out, "head", 1, 0, tiled=True)
    order = []
    bit = 4
    while bit < n_ctx:
        order.append(bit)
        bit *= 2
    order = tuple(order + [2, 1])
    picks_got = lax.ppermute(picks, "ctx", flip(order[0]))
    kv_two = lax.ppermute(kv, "ctx", [(i, i + 2) for i in range(n_ctx - 2)])
    kv_core = lax.ppermute(kv, "ctx", flip(1))
    picks = join(run, "stride_join", picks, picks_got)
    picks_got = lax.ppermute(picks, "ctx", flip(order[1]))
    if pair:
        grad_own, grad_out, w_own = run(
            grad_own_kernel, "grad_own", [grad_out, w_out],
            [shape((rows, head_rows), F32), shape(grad_out.shape, BF16), shape((head_rows, width), BF16)],
            [pltpu.SemaphoreType.DMA((8,))], flops=proj, after=[kv_core], far=(0, 1),
        )
    for bit in order[2:-1]:
        picks = join(run, "stride_join", picks, picks_got)
        picks_got = lax.ppermute(picks, "ctx", flip(bit))
    kv_two = run.hold(kv_two)
    kv_two_core = lax.ppermute(kv_two, "ctx", flip(1))

    if pair:
        w_near = run.hold(w_near)
        w_far = lax.ppermute(w_near, "ctx", flip(1))
        grad_other, = run(
            grad_other_kernel, "grad_other", [grad_out, w_near, w_far],
            [shape((rows, head_rows), BF16)], flops=proj,
        )
        grad_got = lax.ppermute(grad_other, "head", swap)

    chunk_rows = (2 * (rows // TILE) + 1) * TILE
    window = pltpu.VMEM((3 * rows, HEAD_SIZE), BF16)
    picked_rows = n_ctx * BLOCK_TOKENS
    pick = pltpu.VMEM((picked_rows, HEAD_SIZE), BF16)
    out, top, total, first = run(
        band_forward_kernel, "band_forward", [stride_offset, queries, kv, kv_core, kv_two, kv_two_core],
        [shape((2, HEAD_SIZE, rows), F32), shape((2, rows), F32), shape((2, rows), F32), shape((2, rows), jnp.int32)],
        [window, window, pltpu.VMEM((chunk_rows, 2 * TILE), F32), pltpu.VMEM((chunk_rows, 2 * TILE), BF16)],
        flops=2 * scores * chunk_rows,
    )
    picks = join(run, "stride_join", picks, picks_got)
    picks_other = lax.ppermute(picks, "ctx", flip(1))
    if not pair:
        grad_all = mm(grad_out, w_all, NT).astype(BF16)
        grad_all = lax.all_to_all(grad_all.reshape(rows, n_head, head_rows), "head", 1, 0, tiled=True)
        grad_all = grad_all.reshape(n_head, rows, head_rows).astype(F32)
        grad_own = jnp.sum(grad_all, axis=0)
        grad_got = jnp.zeros((rows, head_rows), BF16)
    if pair:
        grad_got = run.hold(grad_got, "hold_grad")
    attended, lse = run(
        functools.partial(stride_forward_kernel, order), "stride_forward",
        [first, queries, picks, picks_other, out, top, total],
        [shape((rows, head_rows), BF16), shape((2, rows), F32)],
        [pltpu.VMEM((2, picked_rows, HEAD_SIZE), BF16)] * 2
        + [pltpu.VMEM((rows // TILE, picked_rows, 2 * TILE), F32), pltpu.VMEM((rows // TILE, picked_rows, 2 * TILE), BF16)],
        flops=2 * scores * picked_rows,
    )
    if pair:
        att_other = lax.ppermute(attended, "head", swap)
        bits = [1]
        while 2 * bits[-1] < ratio:
            bits.append(2 * bits[-1])
        own_bits = tuple(bits[:1] + bits[:0:-1])
        other_bits = own_bits

        def weight_grad(source, name, bits):
            part = shape((ratio // 2, head_rows, cols), BF16)
            return run(
                functools.partial(weight_grad_kernel, bits), name, [source, grad_out], [part, part], flops=proj
            )

        own_keep, own_send = weight_grad(attended, "weight_grad_own", own_bits)
        own_got = lax.ppermute(own_send, "ctx", flip(1))
    if pair:
        own_keep, own_send = halve(run, "weight_grad_own_core", own_keep, own_got)
        own_got = lax.ppermute(own_send, "ctx", flip(own_bits[1]))
    grad_att, row_dot, grad_q, stride_keep, stride_send = run(
        functools.partial(stride_backward_kernel, order), "stride_backward",
        [first, queries, grad_own, grad_got, attended, lse, picks, picks_other],
        [
            shape((rows, head_rows), BF16), shape((2, rows), F32), shape((2, HEAD_SIZE, rows), F32),
            shape(picks.shape, BF16), shape(picks.shape, BF16),
        ],
        [
            pick, pick, pltpu.VMEM((picked_rows, rows), BF16), pltpu.VMEM((picked_rows, rows), BF16),
            pltpu.VMEM((picked_rows, 2 * TILE), F32), pltpu.VMEM((picked_rows, 2 * TILE), F32),
        ],
        flops=5 * scores * picked_rows,
    )
    stride_got = lax.ppermute(stride_send, "ctx", flip(1))
    if pair:
        other_keep, other_send = weight_grad(att_other, "weight_grad_other", other_bits)
        other_got = lax.ppermute(other_send, "ctx", flip(1))
    if pair:
        for bit in own_bits[2:]:
            own_keep, own_send = halve(run, "weight_grad_own_low", own_keep, own_got)
            own_got = lax.ppermute(own_send, "ctx", flip(bit))
    if pair:
        other_keep, other_send = halve(run, "weight_grad_other_core", other_keep, other_got)
        other_got = lax.ppermute(other_send, "ctx", flip(other_bits[1]))
    stride_keep, stride_send = halve(run, "stride_core", stride_keep, stride_got)
    stride_got = lax.ppermute(stride_send, "ctx", flip(2))
    grad_queries, own, one, two = run(
        band_backward_kernel, "band_backward",
        [queries, grad_att, kv, kv_core, kv_two, kv_two_core, lse, row_dot, grad_q],
        [shape((rows, head_rows), BF16)] + [shape((2 * rows, HEAD_SIZE), BF16)] * 3,
        [
            window, window, pltpu.VMEM((3 * rows, HEAD_SIZE), F32), pltpu.VMEM((3 * rows, HEAD_SIZE), F32),
            pltpu.VMEM((chunk_rows, 2 * TILE), BF16), pltpu.VMEM((chunk_rows, 2 * TILE), BF16),
        ],
        flops=5 * scores * chunk_rows,
    )
    one_got = lax.ppermute(one, "ctx", flip(1))
    stride_bits = list(reversed(order))[1:]
    if pair:
        for bit in other_bits[2:]:
            other_keep, other_send = halve(run, "weight_grad_other_low", other_keep, other_got)
            other_got = lax.ppermute(other_send, "ctx", flip(bit))
    stride_keep, stride_send = halve(run, "stride_y", stride_keep, stride_got)
    stride_got = lax.ppermute(stride_send, "ctx", flip(stride_bits[1]))
    if pair:
        block = (head_rows, cols)
        own_low, = run(end_kernel, "weight_grad_own_end", [own_keep, own_got], [shape(block, BF16)])
    if pair:
        other_low, = run(end_kernel, "weight_grad_other_end", [other_keep, other_got], [shape(block, BF16)])
        other_got = lax.ppermute(other_low, "head", swap)
        two, = run(functools.partial(add_kernel, 1), "band_two", [two, one_got], [shape(two.shape, BF16)])
        two_got = lax.ppermute(two, "ctx", [(i + 2, i) for i in range(n_ctx - 2)])
        layer_out, = run(
            layer_out_kernel, "layer_out", [attended, att_other, w_own, w_near, w_far],
            [shape((rows, width), BF16)], flops=2 * proj,
        )
        sum_keep, sum_send = run(
            choose_kernel, "choose", [own_low, other_got], [shape(block, BF16)] * 2
        )
        sum_got = lax.ppermute(sum_send, "ctx", flip(n_ctx // 2))
        for bit in stride_bits[2:]:
            stride_keep, stride_send = halve(run, "stride_z", stride_keep, stride_got)
            stride_got = lax.ppermute(stride_send, "ctx", flip(bit))
    else:
        two, = run(functools.partial(add_kernel, 1), "band_two", [two, one_got], [shape(two.shape, BF16)])
        two_got = lax.ppermute(two, "ctx", [(i + 2, i) for i in range(n_ctx - 2)])
        for bit in stride_bits[2:]:
            stride_keep, stride_send = halve(run, "stride_z", stride_keep, stride_got)
            stride_got = lax.ppermute(stride_send, "ctx", flip(bit))
        att_all = lax.all_gather(attended, "head", axis=1, tiled=True)
        layer_out = mm(att_all, w_all).astype(BF16)
        terms = mm(att_all, grad_out, TN).astype(BF16).reshape(n_head, head_rows, ratio, cols)
        terms = jnp.transpose(terms, (0, 2, 1, 3)).reshape(n_ctx, head_rows, cols)
        terms = lax.psum_scatter(terms, "ctx", scatter_dimension=0, tiled=True)[0]
        route = []
        for c in range(n_ctx):
            for h in range(n_head):
                target = (h * ratio + c % ratio) * n_head + c // ratio
                route.append((c * n_head + h, target))
        grad_w_out = lax.ppermute(terms, ("ctx", "head"), route)

    key_gradient, value_gradient = run(
        finish_kernel, "finish", [stride_offset, own, one_got, two_got, stride_keep, stride_got],
        [shape((rows, HEAD_SIZE), BF16)] * 2,
        [pltpu.VMEM((2 * rows, HEAD_SIZE), F32)],
    )
    if pair:
        grad_w_out, = run(last_sum_kernel, "last_sum", [sum_keep, sum_got], [shape(block, BF16)])
    return (layer_out, grad_queries, key_gradient, value_gradient, grad_w_out)


def solution(mesh):
    placed = (
        P("ctx", "head"),
        P("ctx", "head"),
        P("ctx", "head"),
        P("head"),
        P("head", None),
        P("ctx", "head"),
    )
    return jax.shard_map(
        body,
        mesh=mesh,
        in_specs=placed,
        out_specs=(
            P("ctx", "head"),
            P("ctx", "head"),
            P("ctx", "head"),
            P("ctx", "head"),
            P("head", "ctx"),
        ),
        check_vma=False,
    )
```

```python
import functools
import math

import jax
import jax.numpy as jnp
from jax import lax
from jax.experimental import pallas as pl
from jax.experimental.pallas import tpu as pltpu
from jax.sharding import PartitionSpec as P

HEAD_SIZE = 128
BLOCK_TOKENS = 64
LOCAL = 16
STRIDE = 8
TILE = 128
BF16 = jnp.bfloat16
F32 = jnp.float32
SCALE = HEAD_SIZE ** (-0.5)
EXP2_SCALE = SCALE * math.log2(math.e)
MASKED = -1e30

VMEM = pl.BlockSpec(memory_space=pltpu.VMEM)
ANY = pl.BlockSpec(memory_space=pl.ANY)
HBM = pl.BlockSpec(memory_space=pltpu.HBM)
SMEM = pl.BlockSpec(memory_space=pltpu.SMEM)
NN = (((1,), (0,)), ((), ()))
NT = (((1,), (1,)), ((), ()))
TN = (((0,), (0,)), ((), ()))


def mm(left, right, dims=NN):
    return lax.dot_general(left, right, dims, preferred_element_type=F32)


USEC = {'pack': 2, 'grad_own': 2, 'grad_other': 0.1, 'band_forward': 2.7, 'stride_forward': 36, 'stride_backward': 46, 'band_backward': 40, 'layer_out': 26, 'finish': 0.1, 'last_sum': 7, 'weight_grad_own': 8, 'weight_grad_other': 8, 'hold_grad': 10, 'weight_grad_own_low': 10}


class Sequence:
    def __init__(self):
        self.last = []

    def __call__(self, kernel, name, ins, out_shapes, scratch=(), mib=32, flops=0, after=(), far=(), out_space=VMEM):
        extra = self.last + list(after)
        count = len(ins)

        def wrapped(*refs):
            rest = refs[count + len(extra) :]
            kernel(*refs[:count], *rest[: len(out_shapes)], *rest[len(out_shapes) + 1 :])
            token = rest[len(out_shapes)]
            token[...] = jnp.zeros_like(token)

        specs = [SMEM if a.ndim == 1 else VMEM for a in ins]
        for index in far:
            specs[index] = HBM
        outs = pl.pallas_call(
            wrapped,
            name=name,
            out_shape=list(out_shapes) + [shape((8, 128), F32)],
            in_specs=specs + [ANY] * len(extra),
            out_specs=[out_space] * len(out_shapes) + [VMEM],
            scratch_shapes=list(scratch),
            compiler_params=pltpu.CompilerParams(vmem_limit_bytes=mib * 2**20),
            cost_estimate=pl.CostEstimate(flops=int(1e9 * USEC.get(name, 0.1)), bytes_accessed=1, transcendentals=0),
        )(*ins, *extra)
        self.last = [outs[-1]]
        return outs[:-1]


    def hold(self, array, name="hold"):
        extra = self.last

        def kernel(*refs):
            token = refs[-1]
            token[...] = jnp.zeros_like(token)

        held, token = pl.pallas_call(
            kernel,
            name=name,
            out_shape=[shape(array.shape, array.dtype), shape((8, 128), F32)],
            in_specs=[ANY] * (1 + len(extra)),
            out_specs=[ANY, VMEM],
            input_output_aliases={0: 0},
            compiler_params=pltpu.CompilerParams(vmem_limit_bytes=2**20),
            cost_estimate=pl.CostEstimate(flops=int(1e9 * USEC.get(name, 0.1)), bytes_accessed=1, transcendentals=0),
        )(array, *extra)
        self.last = [token]
        return held


def shape(dims, dtype):
    return jax.ShapeDtypeStruct(dims, dtype)


def flips(count, bit):
    return [(i, i ^ bit) for i in range(count)]


def slot_owner(ctx, slot, order):
    mask = 0
    for k, bit in enumerate(order):
        if slot >> k & 1:
            mask |= bit
    return ctx ^ mask


def run_copies(pairs, sem):
    copies = [pltpu.make_async_copy(src, dst, sem.at[i]) for i, (src, dst) in enumerate(pairs)]
    for copy in copies:
        copy.start()
    return copies


def pack_kernel(phase_ref, k_ref, v_ref, *refs):
    if len(refs) == 4:
        kv_ref, pick_ref, phases, sem = refs
        pairs = []
    else:
        w_ref, kv_ref, pick_ref, piece_ref, phases, sem = refs
        cols = piece_ref.shape[1]
        start = (1 - lax.axis_index("head")) * 2 * cols + lax.axis_index("ctx") % 2 * cols
        pairs = [(w_ref.at[:, pl.ds(pl.multiple_of(start, cols), cols)], piece_ref)]
    rows = k_ref.shape[0]
    pairs = [(phase_ref, phases), (k_ref, kv_ref.at[pl.ds(0, rows)]), (v_ref, kv_ref.at[pl.ds(rows, rows)])] + pairs
    copies = run_copies(pairs, sem)
    for copy in copies[:3]:
        copy.wait()
    for r in range(2):
        for part in range(2):
            start = pl.multiple_of(part * rows + (STRIDE - 1 - phases[r]) * BLOCK_TOKENS, BLOCK_TOKENS)
            at = (2 * r + part) * BLOCK_TOKENS
            pick_ref[at : at + BLOCK_TOKENS] = kv_ref[pl.ds(start, BLOCK_TOKENS)]
    for copy in copies[3:]:
        copy.wait()


def join_kernel(first_ref, second_ref, out_ref):
    middle = first_ref.shape[0]
    out_ref[:middle] = first_ref[...]
    out_ref[middle:] = second_ref[...]


def join(run, name, first, second, after=()):
    return run(join_kernel, name, [first, second], [shape((2 * first.shape[0],) + first.shape[1:], BF16)], after=after)[0]


def load_window(core, own_ref, core_ref, two_ref, two_core_ref, part, out):
    rows = own_ref.shape[0] // 2
    piece = pl.ds(part * rows, rows)
    out[:rows] = two_ref[piece]
    out[rows : 2 * rows] = jnp.where(core == 0, two_core_ref[piece], core_ref[piece])
    out[2 * rows :] = own_ref[piece]


def band_scores(ctx, tile, chunk, tiles, k_win, q_tile):
    start = (tile + chunk) * TILE
    s = mm(k_win[start : start + TILE], q_tile, NT)
    if chunk == 0 or chunk == 2 * tiles:
        key = lax.broadcasted_iota(jnp.int32, s.shape, 0)
        token = lax.broadcasted_iota(jnp.int32, s.shape, 1) % TILE
        if chunk == 0:
            s = jnp.where(key // BLOCK_TOKENS > token // BLOCK_TOKENS, s, MASKED)
        else:
            s = jnp.where(key <= token, s, MASKED)
    if tile + chunk < 2 * tiles:
        first = 2 - (tile + chunk) // tiles
        s = jnp.where(ctx >= first, s, MASKED)
    return s


def both_heads(ref, tile):
    rows = slice(tile * TILE, (tile + 1) * TILE)
    return jnp.concatenate([ref[rows, :HEAD_SIZE], ref[rows, HEAD_SIZE:]], axis=0)


def band_forward_kernel(phase_ref, q_ref, own_ref, core_ref, two_ref, two_core_ref, out_ref, max_ref, sum_ref, first_ref, k_win, v_win, s_buf, p_buf):
    ctx = lax.axis_index("ctx")
    core = ctx % 2
    tiles = q_ref.shape[0] // TILE
    chunks = 2 * tiles + 1
    load_window(core, own_ref, core_ref, two_ref, two_core_ref, 0, k_win)
    load_window(core, own_ref, core_ref, two_ref, two_core_ref, 1, v_win)
    for r in range(2):
        first_ref[r : r + 1, :] = jnp.full((1, first_ref.shape[1]), (STRIDE - 1 - phase_ref[r]) * BLOCK_TOKENS, jnp.int32)
    for tile in range(tiles):
        q_tile = both_heads(q_ref, tile)
        top = None
        for chunk in range(chunks):
            s = band_scores(ctx, tile, chunk, tiles, k_win, q_tile)
            s_buf[chunk * TILE : (chunk + 1) * TILE] = s
            here = jnp.max(s.reshape(TILE // 8, 8, 2 * TILE), axis=0)
            top = here if top is None else jnp.maximum(top, here)
        top = jnp.max(top, axis=0, keepdims=True)
        total = None
        for chunk in range(chunks):
            p = jnp.exp2((s_buf[chunk * TILE : (chunk + 1) * TILE] - top) * EXP2_SCALE)
            here = jnp.sum(p.reshape(TILE // 8, 8, 2 * TILE), axis=0)
            total = here if total is None else total + here
            p_buf[chunk * TILE : (chunk + 1) * TILE] = p.astype(BF16)
        total = jnp.sum(total, axis=0, keepdims=True)
        out = mm(v_win[tile * TILE : (tile + chunks) * TILE], p_buf[...], TN)
        at = slice(tile * TILE, (tile + 1) * TILE)
        for r in range(2):
            half = slice(r * TILE, (r + 1) * TILE)
            out_ref[r, :, at] = out[:, half]
            max_ref[r : r + 1, at] = top[:, half]
            sum_ref[r : r + 1, at] = total[:, half]


def band_backward_kernel(
    q_ref, do_ref, own_ref, core_ref, two_ref, two_core_ref, lse_ref, dot_ref, dq_in_ref,
    dq_ref, own_out, one_out, two_out, k_win, v_win, dk_acc, dv_acc, p_buf, ds_buf,
):
    ctx = lax.axis_index("ctx")
    core = ctx % 2
    rows = q_ref.shape[0]
    tiles = rows // TILE
    chunks = 2 * tiles + 1
    load_window(core, own_ref, core_ref, two_ref, two_core_ref, 0, k_win)
    load_window(core, own_ref, core_ref, two_ref, two_core_ref, 1, v_win)
    dk_acc[...] = jnp.zeros_like(dk_acc)
    dv_acc[...] = jnp.zeros_like(dv_acc)
    for tile in range(tiles):
        q_tile = both_heads(q_ref, tile)
        do_tile = both_heads(do_ref, tile)
        at = slice(tile * TILE, (tile + 1) * TILE)
        lse = jnp.concatenate([lse_ref[0:1, at], lse_ref[1:2, at]], axis=1)
        dot = jnp.concatenate([dot_ref[0:1, at], dot_ref[1:2, at]], axis=1)
        for chunk in range(chunks):
            s = band_scores(ctx, tile, chunk, tiles, k_win, q_tile)
            p = jnp.exp2((s - lse) * EXP2_SCALE)
            start = (tile + chunk) * TILE
            dp = mm(v_win[start : start + TILE], do_tile, NT)
            piece = slice(chunk * TILE, (chunk + 1) * TILE)
            p_buf[piece] = p.astype(BF16)
            ds_buf[piece] = (p * (dp - dot)).astype(BF16)
        window = slice(tile * TILE, (tile + chunks) * TILE)
        dv_acc[window] += mm(p_buf[...], do_tile)
        dk_acc[window] += mm(ds_buf[...], q_tile)
        dq = mm(k_win[window], ds_buf[...], TN)
        for r in range(2):
            whole = (dq[:, r * TILE : (r + 1) * TILE] + dq_in_ref[r, :, at]) * SCALE
            dq_ref[at, r * HEAD_SIZE : (r + 1) * HEAD_SIZE] = whole.T.astype(BF16)
    for index, out in ((0, two_out), (1, one_out), (2, own_out)):
        part = slice(index * rows, (index + 1) * rows)
        out[:rows] = (dk_acc[part] * SCALE).astype(BF16)
        out[rows:] = dv_acc[part].astype(BF16)


def load_picked(mine_ref, other_ref, r, part, out):
    size = 4 * BLOCK_TOKENS
    slots = mine_ref.shape[0] // size
    for slot in range(2 * slots):
        source = mine_ref if slot < slots else other_ref
        start = (slot % slots) * size + (2 * r + part) * BLOCK_TOKENS
        out[slot * BLOCK_TOKENS : (slot + 1) * BLOCK_TOKENS] = source[start : start + BLOCK_TOKENS]


def slot_scores(ctx, slot, order, nearest, token_start, s):
    owner = slot_owner(ctx, slot, order)
    token = token_start + lax.broadcasted_iota(jnp.int32, s.shape, 1)
    first = jnp.where(owner < ctx - 2, 0, jnp.where(owner == ctx - 2, nearest, 2**30))
    return jnp.where(token >= first, s, MASKED)


def stride_forward_kernel(order, first_ref, q_ref, mine_ref, other_ref, out_in_ref, max_in_ref, sum_in_ref, att_ref, lse_ref, k_pick, v_pick, s_buf, p_buf):
    ctx = lax.axis_index("ctx")
    rows = q_ref.shape[0]
    slots = k_pick.shape[1] // BLOCK_TOKENS
    width = 2 * TILE
    steps = [(r, token_start) for r in range(2) for token_start in range(0, rows, width)]
    for r in range(2):
        load_picked(mine_ref, other_ref, r, 0, k_pick.at[r])
        load_picked(mine_ref, other_ref, r, 1, v_pick.at[r])

    def scores(step):
        r, token_start = steps[step]
        q_tile = q_ref[token_start : token_start + width, r * HEAD_SIZE : (r + 1) * HEAD_SIZE]
        s_buf[step] = mm(k_pick[r], q_tile, NT)

    def weigh(step):
        r, token_start = steps[step]
        at = slice(token_start, token_start + width)
        old = max_in_ref[r : r + 1, at]
        top = None
        for slot in range(slots):
            piece = slice(slot * BLOCK_TOKENS, (slot + 1) * BLOCK_TOKENS)
            s = slot_scores(ctx, slot, order, first_ref[r : r + 1, at], token_start, s_buf[step, piece])
            s_buf[step, piece] = s
            here = jnp.max(s.reshape(BLOCK_TOKENS // 8, 8, width), axis=0)
            top = here if top is None else jnp.maximum(top, here)
        top = jnp.maximum(jnp.max(top, axis=0, keepdims=True), old)
        total = None
        for slot in range(slots):
            piece = slice(slot * BLOCK_TOKENS, (slot + 1) * BLOCK_TOKENS)
            p = jnp.exp2((s_buf[step, piece] - top) * EXP2_SCALE)
            here = jnp.sum(p.reshape(BLOCK_TOKENS // 8, 8, width), axis=0)
            total = here if total is None else total + here
            p_buf[step, piece] = p.astype(BF16)
        factor = jnp.exp2((old - top) * EXP2_SCALE)
        total = jnp.sum(total, axis=0, keepdims=True) + sum_in_ref[r : r + 1, at] * factor
        lse_ref[r : r + 1, at] = top + jnp.log2(total) * (1.0 / EXP2_SCALE)
        return factor, total

    def mix(step, factor, total):
        r, token_start = steps[step]
        at = slice(token_start, token_start + width)
        out = mm(v_pick[r], p_buf[step], TN) + out_in_ref[r, :, at] * factor
        att_ref[at, r * HEAD_SIZE : (r + 1) * HEAD_SIZE] = (out / total).T.astype(BF16)

    scores(0)
    for step in range(len(steps)):
        if step + 1 < len(steps):
            scores(step + 1)
        mix(step, *weigh(step))


def stride_backward_kernel(order, first_ref, q_ref, grad_own_ref, grad_got_ref, att_ref, lse_ref, mine_ref, other_ref, do_ref, dot_ref, dq_ref, keep_ref, send_ref, k_pick, v_pick, p_buf, ds_buf, s_buf, dp_buf):
    ctx = lax.axis_index("ctx")
    rows = q_ref.shape[0]
    slots = k_pick.shape[1] // BLOCK_TOKENS
    width = 2 * TILE
    size = 4 * BLOCK_TOKENS
    do_ref[...] = (grad_own_ref[...] + grad_got_ref[...].astype(F32)).astype(BF16)
    for r in range(2):
        head = slice(r * HEAD_SIZE, (r + 1) * HEAD_SIZE)
        product = do_ref[:, head].astype(F32) * att_ref[:, head].astype(F32)
        dot_ref[r : r + 1, :] = jnp.sum(product.T, axis=0, keepdims=True)
        load_picked(mine_ref, other_ref, r, 0, k_pick.at[r])
        load_picked(mine_ref, other_ref, r, 1, v_pick.at[r])
    steps = [(r, token_start) for r in range(2) for token_start in range(0, rows, width)]

    def products(step):
        r, token_start = steps[step]
        at = slice(token_start, token_start + width)
        head = slice(r * HEAD_SIZE, (r + 1) * HEAD_SIZE)
        s_buf[step] = mm(k_pick[r], q_ref[at, head], NT)
        dp_buf[step] = mm(v_pick[r], do_ref[at, head], NT)

    def weigh(step):
        r, token_start = steps[step]
        at = slice(token_start, token_start + width)
        lse = lse_ref[r : r + 1, at]
        dot = dot_ref[r : r + 1, at]
        for slot in range(slots):
            piece = slice(slot * BLOCK_TOKENS, (slot + 1) * BLOCK_TOKENS)
            s = slot_scores(ctx, slot, order, first_ref[r : r + 1, at], token_start, s_buf[step, piece])
            p = jnp.exp2((s - lse) * EXP2_SCALE)
            p_buf[r, piece, at] = p.astype(BF16)
            ds_buf[r, piece, at] = (p * (dp_buf[step, piece] - dot)).astype(BF16)

    products(0)
    for step, (r, token_start) in enumerate(steps):
        if step + 1 < len(steps):
            products(step + 1)
        weigh(step)
        if token_start + width < rows:
            continue
        head = slice(r * HEAD_SIZE, (r + 1) * HEAD_SIZE)
        dv = mm(p_buf[r], do_ref[:, head])
        dk = mm(ds_buf[r], q_ref[:, head]) * SCALE
        dq_ref[r] = mm(k_pick[r], ds_buf[r], TN)
        for slot in range(slots):
            target = keep_ref if slot < slots // 2 else send_ref
            start = (slot % (slots // 2)) * size + 2 * r * BLOCK_TOKENS
            piece = slice(slot * BLOCK_TOKENS, (slot + 1) * BLOCK_TOKENS)
            target[start : start + BLOCK_TOKENS] = dk[piece].astype(BF16)
            target[start + BLOCK_TOKENS : start + 2 * BLOCK_TOKENS] = dv[piece].astype(BF16)


def finish_kernel(phase_ref, own_ref, core_ref, two_ref, stride_a_ref, stride_b_ref, dk_ref, dv_ref, acc):
    even = lax.axis_index("ctx") % 2 == 0
    rows = dk_ref.shape[0]
    acc[...] = own_ref[...].astype(F32) + two_ref[...].astype(F32) + jnp.where(even, core_ref[...].astype(F32), 0.0)
    stride = stride_a_ref[...].astype(F32) + stride_b_ref[...].astype(F32)
    for r in range(2):
        for part in range(2):
            start = pl.multiple_of(part * rows + (STRIDE - 1 - phase_ref[r]) * BLOCK_TOKENS, BLOCK_TOKENS)
            at = (2 * r + part) * BLOCK_TOKENS
            acc[pl.ds(start, BLOCK_TOKENS)] += stride[at : at + BLOCK_TOKENS]
    dk_ref[...] = acc[:rows].astype(BF16)
    dv_ref[...] = acc[rows:].astype(BF16)


def grad_own_kernel(g_ref, w_ref, out_ref, g_out, w_own, sem):
    width = g_ref.shape[1]
    start = lax.axis_index("head") * width
    step = width // 4
    pairs = []
    for at in range(0, width, step):
        cols = pl.ds(at, step)
        pairs.append((g_ref.at[:, cols], g_out.at[:, cols]))
        pairs.append((w_ref.at[:, pl.ds(pl.multiple_of(start + at, step), step)], w_own.at[:, cols]))
    copies = run_copies(pairs, sem)
    total = None
    for index in range(4):
        copies[2 * index].wait()
        copies[2 * index + 1].wait()
        cols = slice(index * step, (index + 1) * step)
        term = mm(g_out[:, cols], w_own[:, cols], NT)
        total = term if total is None else total + term
    out_ref[...] = total


def grad_other_kernel(g_ref, near_ref, far_ref, out_ref):
    core = lax.axis_index("ctx") % 2
    width = near_ref.shape[1]
    near = pl.ds(pl.multiple_of(core * width, width), width)
    far = pl.ds(pl.multiple_of((1 - core) * width, width), width)
    total = mm(g_ref[:, near], near_ref[...], NT) + mm(g_ref[:, far], far_ref[...], NT)
    out_ref[...] = total.astype(BF16)


def layer_out_kernel(own_ref, other_ref, w_ref, near_ref, far_ref, out_ref):
    core = lax.axis_index("ctx") % 2
    width = near_ref.shape[1]
    step = min(width, 256)
    for part, source in ((core, near_ref), (1 - core, far_ref)):
        for at in range(0, width, step):
            cols = pl.ds(pl.multiple_of(part * width + at, step), step)
            total = mm(own_ref[...], w_ref[:, cols]) + mm(other_ref[...], source[:, at : at + step])
            out_ref[:, cols] = total.astype(BF16)


def weight_grad_kernel(bits, att_ref, g_ref, keep_ref, send_ref):
    ctx = lax.axis_index("ctx")
    _, _, cols = keep_ref.shape
    blocks = 1 << len(bits)
    att = att_ref[...].T
    for slot in range(blocks):
        mask = 0
        for k, bit in enumerate(bits):
            if slot >> (len(bits) - 1 - k) & 1:
                mask |= bit
        block = (ctx % blocks) ^ mask
        term = mm(att, g_ref[:, pl.ds(pl.multiple_of(block * cols, cols), cols)]).astype(BF16)
        if slot < blocks // 2:
            keep_ref[slot] = term
        else:
            send_ref[slot - blocks // 2] = term


def halve_kernel(keep_ref, got_ref, keep_out, send_out):
    middle = keep_out.shape[0]
    keep_out[...] = keep_ref[:middle].astype(F32) + got_ref[:middle].astype(F32)
    send_out[...] = (keep_ref[middle:].astype(F32) + got_ref[middle:].astype(F32)).astype(BF16)


def halve(run, name, keep, got, after=()):
    half = (keep.shape[0] // 2,) + keep.shape[1:]
    return run(halve_kernel, name, [keep, got], [shape(half, F32), shape(half, BF16)], after=after)


def add_kernel(core, left_ref, right_ref, out_ref):
    here = lax.axis_index("ctx") % 2 == core
    left = left_ref[...].astype(F32)
    out_ref[...] = jnp.where(here, left + right_ref[...].astype(F32), left).astype(BF16)


def end_kernel(left_ref, right_ref, low_ref):
    low_ref[...] = (left_ref[0].astype(F32) + right_ref[0].astype(F32)).astype(BF16)


def choose_kernel(own_ref, other_ref, keep_ref, send_ref):
    same = lax.axis_index("ctx") // (lax.axis_size("ctx") // 2) == lax.axis_index("head")
    keep_ref[...] = jnp.where(same, own_ref[...], other_ref[...])
    send_ref[...] = jnp.where(same, other_ref[...], own_ref[...])


def last_sum_kernel(keep_ref, got_ref, out_ref):
    out_ref[...] = (keep_ref[...].astype(F32) + got_ref[...].astype(F32)).astype(BF16)


def body(queries, rotated_key_rows, value_head_rows, stride_offset, w_out, grad_out):
    rows = queries.shape[0]
    n_ctx = lax.axis_size("ctx")
    n_head = lax.axis_size("head")
    model = w_out.shape[1]
    width = grad_out.shape[1]
    head_rows = w_out.shape[0]
    ratio = n_ctx // n_head
    cols = model // n_ctx
    pair = n_head == 2
    flip = functools.partial(flips, n_ctx)
    swap = [(0, 1), (1, 0)]
    scores = rows * 2 * HEAD_SIZE * 2
    proj = 2 * rows * head_rows * width
    run = Sequence()

    packed = run(
        pack_kernel, "pack",
        [stride_offset, rotated_key_rows, value_head_rows] + ([w_out] if pair else []),
        [shape((2 * rows, HEAD_SIZE), BF16), shape((4 * BLOCK_TOKENS, HEAD_SIZE), BF16)]
        + ([shape((head_rows, width // 2), BF16)] if pair else []),
        [pltpu.SMEM((2,), jnp.int32), pltpu.SemaphoreType.DMA((4,))], far=(0, 1, 2, 3) if pair else (0, 1, 2), mib=54,
    )
    run.last = []
    kv, picks = packed[:2]
    if pair:
        w_near = lax.ppermute(packed[2], "head", swap)
    else:
        w_all = lax.all_to_all(w_out, "head", 1, 0, tiled=True)
    order = []
    bit = 4
    while bit < n_ctx:
        order.append(bit)
        bit *= 2
    order = tuple(order + [2, 1])
    picks_got = lax.ppermute(picks, "ctx", flip(order[0]))
    kv_two = lax.ppermute(kv, "ctx", [(i, i + 2) for i in range(n_ctx - 2)])
    kv_core = lax.ppermute(kv, "ctx", flip(1))
    picks = join(run, "stride_join", picks, picks_got)
    picks_got = lax.ppermute(picks, "ctx", flip(order[1]))
    if pair:
        grad_own, grad_out, w_own = run(
            grad_own_kernel, "grad_own", [grad_out, w_out],
            [shape((rows, head_rows), F32), shape(grad_out.shape, BF16), shape((head_rows, width), BF16)],
            [pltpu.SemaphoreType.DMA((8,))], flops=proj, after=[kv_core], far=(0, 1),
        )
    for bit in order[2:-1]:
        picks = join(run, "stride_join", picks, picks_got)
        picks_got = lax.ppermute(picks, "ctx", flip(bit))
    kv_two = run.hold(kv_two)
    kv_two_core = lax.ppermute(kv_two, "ctx", flip(1))

    if pair:
        w_near = run.hold(w_near)
        w_far = lax.ppermute(w_near, "ctx", flip(1))
        grad_other, = run(
            grad_other_kernel, "grad_other", [grad_out, w_near, w_far],
            [shape((rows, head_rows), BF16)], flops=proj,
        )
        grad_got = lax.ppermute(grad_other, "head", swap)

    chunk_rows = (2 * (rows // TILE) + 1) * TILE
    window = pltpu.VMEM((3 * rows, HEAD_SIZE), BF16)
    picked_rows = n_ctx * BLOCK_TOKENS
    pick = pltpu.VMEM((picked_rows, HEAD_SIZE), BF16)
    out, top, total, first = run(
        band_forward_kernel, "band_forward", [stride_offset, queries, kv, kv_core, kv_two, kv_two_core],
        [shape((2, HEAD_SIZE, rows), F32), shape((2, rows), F32), shape((2, rows), F32), shape((2, rows), jnp.int32)],
        [window, window, pltpu.VMEM((chunk_rows, 2 * TILE), F32), pltpu.VMEM((chunk_rows, 2 * TILE), BF16)],
        flops=2 * scores * chunk_rows,
    )
    picks = join(run, "stride_join", picks, picks_got)
    picks_other = lax.ppermute(picks, "ctx", flip(1))
    if not pair:
        grad_all = mm(grad_out, w_all, NT).astype(BF16)
        grad_all = lax.all_to_all(grad_all.reshape(rows, n_head, head_rows), "head", 1, 0, tiled=True)
        grad_all = grad_all.reshape(n_head, rows, head_rows).astype(F32)
        grad_own = jnp.sum(grad_all, axis=0)
        grad_got = jnp.zeros((rows, head_rows), BF16)
    if pair:
        grad_got = run.hold(grad_got, "hold_grad")
    attended, lse = run(
        functools.partial(stride_forward_kernel, order), "stride_forward",
        [first, queries, picks, picks_other, out, top, total],
        [shape((rows, head_rows), BF16), shape((2, rows), F32)],
        [pltpu.VMEM((2, picked_rows, HEAD_SIZE), BF16)] * 2
        + [pltpu.VMEM((rows // TILE, picked_rows, 2 * TILE), F32), pltpu.VMEM((rows // TILE, picked_rows, 2 * TILE), BF16)],
        flops=2 * scores * picked_rows,
    )
    if pair:
        att_other = lax.ppermute(attended, "head", swap)
        bits = [1]
        while 2 * bits[-1] < ratio:
            bits.append(2 * bits[-1])
        own_bits = tuple(bits[:1] + bits[:0:-1])
        other_bits = own_bits

        def weight_grad(source, name, bits):
            part = shape((ratio // 2, head_rows, cols), BF16)
            return run(
                functools.partial(weight_grad_kernel, bits), name, [source, grad_out], [part, part], flops=proj
            )

        own_keep, own_send = weight_grad(attended, "weight_grad_own", own_bits)
        own_got = lax.ppermute(own_send, "ctx", flip(1))
    if pair:
        own_keep, own_send = halve(run, "weight_grad_own_core", own_keep, own_got)
        own_got = lax.ppermute(own_send, "ctx", flip(own_bits[1]))
    grad_att, row_dot, grad_q, stride_keep, stride_send = run(
        functools.partial(stride_backward_kernel, order), "stride_backward",
        [first, queries, grad_own, grad_got, attended, lse, picks, picks_other],
        [
            shape((rows, head_rows), BF16), shape((2, rows), F32), shape((2, HEAD_SIZE, rows), F32),
            shape(picks.shape, BF16), shape(picks.shape, BF16),
        ],
        [pltpu.VMEM((2, picked_rows, HEAD_SIZE), BF16)] * 2
        + [pltpu.VMEM((2, picked_rows, rows), BF16)] * 2
        + [pltpu.VMEM((rows // TILE, picked_rows, 2 * TILE), F32)] * 2,
        mib=min(60, 2 * n_ctx),
        flops=5 * scores * picked_rows,
    )
    stride_got = lax.ppermute(stride_send, "ctx", flip(1))
    if pair:
        other_keep, other_send = weight_grad(att_other, "weight_grad_other", other_bits)
        other_got = lax.ppermute(other_send, "ctx", flip(1))
    if pair:
        for bit in own_bits[2:]:
            own_keep, own_send = halve(run, "weight_grad_own_low", own_keep, own_got)
            own_got = lax.ppermute(own_send, "ctx", flip(bit))
    if pair:
        other_keep, other_send = halve(run, "weight_grad_other_core", other_keep, other_got)
        other_got = lax.ppermute(other_send, "ctx", flip(other_bits[1]))
    stride_keep, stride_send = halve(run, "stride_core", stride_keep, stride_got)
    stride_got = lax.ppermute(stride_send, "ctx", flip(2))
    grad_queries, own, one, two = run(
        band_backward_kernel, "band_backward",
        [queries, grad_att, kv, kv_core, kv_two, kv_two_core, lse, row_dot, grad_q],
        [shape((rows, head_rows), BF16)] + [shape((2 * rows, HEAD_SIZE), BF16)] * 3,
        [
            window, window, pltpu.VMEM((3 * rows, HEAD_SIZE), F32), pltpu.VMEM((3 * rows, HEAD_SIZE), F32),
            pltpu.VMEM((chunk_rows, 2 * TILE), BF16), pltpu.VMEM((chunk_rows, 2 * TILE), BF16),
        ],
        flops=5 * scores * chunk_rows,
    )
    one_got = lax.ppermute(one, "ctx", flip(1))
    stride_bits = list(reversed(order))[1:]
    if pair:
        for bit in other_bits[2:]:
            other_keep, other_send = halve(run, "weight_grad_other_low", other_keep, other_got)
            other_got = lax.ppermute(other_send, "ctx", flip(bit))
    stride_keep, stride_send = halve(run, "stride_y", stride_keep, stride_got)
    stride_got = lax.ppermute(stride_send, "ctx", flip(stride_bits[1]))
    if pair:
        block = (head_rows, cols)
        own_low, = run(end_kernel, "weight_grad_own_end", [own_keep, own_got], [shape(block, BF16)])
    if pair:
        other_low, = run(end_kernel, "weight_grad_other_end", [other_keep, other_got], [shape(block, BF16)])
        other_got = lax.ppermute(other_low, "head", swap)
        two, = run(functools.partial(add_kernel, 1), "band_two", [two, one_got], [shape(two.shape, BF16)])
        two_got = lax.ppermute(two, "ctx", [(i + 2, i) for i in range(n_ctx - 2)])
        layer_out, = run(
            layer_out_kernel, "layer_out", [attended, att_other, w_own, w_near, w_far],
            [shape((rows, width), BF16)], flops=2 * proj,
        )
        sum_keep, sum_send = run(
            choose_kernel, "choose", [own_low, other_got], [shape(block, BF16)] * 2
        )
        sum_got = lax.ppermute(sum_send, "ctx", flip(n_ctx // 2))
        for bit in stride_bits[2:]:
            stride_keep, stride_send = halve(run, "stride_z", stride_keep, stride_got)
            stride_got = lax.ppermute(stride_send, "ctx", flip(bit))
    else:
        two, = run(functools.partial(add_kernel, 1), "band_two", [two, one_got], [shape(two.shape, BF16)])
        two_got = lax.ppermute(two, "ctx", [(i + 2, i) for i in range(n_ctx - 2)])
        for bit in stride_bits[2:]:
            stride_keep, stride_send = halve(run, "stride_z", stride_keep, stride_got)
            stride_got = lax.ppermute(stride_send, "ctx", flip(bit))
        att_all = lax.all_gather(attended, "head", axis=1, tiled=True)
        layer_out = mm(att_all, w_all).astype(BF16)
        terms = mm(att_all, grad_out, TN).astype(BF16).reshape(n_head, head_rows, ratio, cols)
        terms = jnp.transpose(terms, (0, 2, 1, 3)).reshape(n_ctx, head_rows, cols)
        terms = lax.psum_scatter(terms, "ctx", scatter_dimension=0, tiled=True)[0]
        route = []
        for c in range(n_ctx):
            for h in range(n_head):
                target = (h * ratio + c % ratio) * n_head + c // ratio
                route.append((c * n_head + h, target))
        grad_w_out = lax.ppermute(terms, ("ctx", "head"), route)

    key_gradient, value_gradient = run(
        finish_kernel, "finish", [stride_offset, own, one_got, two_got, stride_keep, stride_got],
        [shape((rows, HEAD_SIZE), BF16)] * 2,
        [pltpu.VMEM((2 * rows, HEAD_SIZE), F32)],
    )
    if pair:
        grad_w_out, = run(last_sum_kernel, "last_sum", [sum_keep, sum_got], [shape(block, BF16)])
    return (layer_out, grad_queries, key_gradient, value_gradient, grad_w_out)


def solution(mesh):
    placed = (
        P("ctx", "head"),
        P("ctx", "head"),
        P("ctx", "head"),
        P("head"),
        P("head", None),
        P("ctx", "head"),
    )
    return jax.shard_map(
        body,
        mesh=mesh,
        in_specs=placed,
        out_specs=(
            P("ctx", "head"),
            P("ctx", "head"),
            P("ctx", "head"),
            P("ctx", "head"),
            P("head", "ctx"),
        ),
        check_vma=False,
    )
```
